512 devices in a mesh: ctx: 32 (over z, core), head: 16 (over x, y).
Axes of the slice: x: 4, y: 4, z: 16, core: 2. Of those that a mesh axis runs over, the one named last changes fastest.
Arguments:
- q_nope: bfloat16 [4096, 8192], P('ctx', 'head'), may hold values from -6 to 6
- q_rope: bfloat16 [4096, 4096], P('ctx', 'head'), may hold values from -80 to 80
- kv_cache: bfloat16 [4096, 576], P('ctx'), may hold values from -180 to 180
- kv_gain: bfloat16 [512], replicated, may hold values from 0.099609375 to 1.8984375
- w_uk: bfloat16 [64, 128, 512], P('head'), may hold values from -0.5 to 0.5
- w_uv: bfloat16 [64, 512, 128], P('head'), may hold values from -0.25 to 0.25
- attn_out: bfloat16 [4096, 8192], P('ctx', 'head'), may hold values from -6 to 6
- d_out: bfloat16 [4096, 8192], P('ctx', 'head'), may hold values from -6 to 6
- span_table: int32 [32, 2], replicated, may hold values from 0 to 63, as said below
Outputs:
- d_q_nope: bfloat16 [4096, 8192], P('ctx', 'head')
- d_q_rope: bfloat16 [4096, 4096], P('ctx', 'head')
- d_cache: float32 [4096, 576], P('ctx')
The draws below stay inside these ranges and needn't reach their ends.
Inputs may be any that keep to these rules, and one draw needn't show every extreme that they name: `span_table`: row d lists the two blocks of 64 positions held by the rows of ctx index d, in this order: a block c below 32, then its mirror 64 - 1 - c. The first column is a permutation.
All inputs are finite; a program needn't handle non-finite values.
Results may differ from the reference program's by a relative error of at most 0.02.
Values may be sent and summed in bfloat16 or wider, within the bound.
A program may use at most 64 MiB of HBM per device.

```python
import jax
import jax.numpy as jnp
from jax import lax

D_LAT = 512
D_ROPE = 64
D_NOPE = 128
D_V = 128
HEADS = 64
TOK_DEV = 128
SPAN = 64
TOKENS = 4096
N_CTX = 32
N_HEAD = 16


def rope_source(key):
    normal_part = jax.random.normal(jax.random.fold_in(key, 101), (TOKENS, D_ROPE), jnp.float32)
    return normal_part


def draw_kv_cache(key, part):
    normal_rope = rope_source(key)
    key = jax.random.fold_in(key, 1)
    rope_part = jnp.clip(normal_rope, -4.0, 4.0)
    latent = jnp.clip(jax.random.normal(jax.random.fold_in(key, 4), (TOKENS, D_LAT), jnp.float32), -4.0, 4.0)
    return jnp.concatenate([latent, rope_part], axis=1).astype(jnp.bfloat16)


def draw_q_rope(key, part):
    key = jax.random.fold_in(key, 5)
    values = jnp.clip(jax.random.normal(jax.random.fold_in(key, 6), (TOKENS, HEADS, D_ROPE), jnp.float32), -4.0, 4.0)
    return values.reshape(TOKENS, HEADS * D_ROPE).astype(jnp.bfloat16)


def draw_span_table(key, part):
    key = jax.random.fold_in(key, 9)
    block_count = TOKENS // TOK_DEV
    order = jax.random.permutation(key, block_count).astype(jnp.int32)
    return jnp.stack([order, 2 * block_count - 1 - order], axis=1).astype(jnp.int32)


def levels(key, shape, shards, low, largest):
    gain, own = 1.0, jax.random.fold_in(key, 6)
    for position, shards_of in shards:
        heights = jnp.exp(jax.random.uniform(jax.random.fold_in(own, position), (shards_of,), jnp.float32, low / len(shards), largest / len(shards)))
        gain = gain * jnp.repeat(heights, shape[position] // shards_of).reshape([-1 if axis == position else 1 for axis in range(len(shape))])
    return gain


def centred(stream_key, shape, scale, bound, shards=(), kind=jnp.bfloat16):
    gain = levels(stream_key, shape, shards, -0.22, 0.18) if shards else 1.0
    result = jax.random.normal(stream_key, shape, jnp.float32) * scale * gain
    return jnp.minimum(jnp.maximum(result, -bound), bound).astype(kind)


def setup_inputs(seed: int = 0) -> dict:
    seeds = jax.random.split(jax.random.key(seed), 10)
    q_nope = centred(seeds[0], (TOKENS, HEADS * D_NOPE), 1.0, 6.0, ((0, 32), (1, 16)))
    q_rope = draw_q_rope(jax.random.fold_in(seeds[9], 71), 0)
    kv_cache = draw_kv_cache(jax.random.fold_in(seeds[9], 71), 0)
    kv_gain = jnp.clip(1.0 + 0.18 * jax.random.normal(seeds[3], (D_LAT,), jnp.float32), 0.099609375, 1.8984375).astype(jnp.bfloat16)
    w_uk = centred(seeds[4], (HEADS, D_NOPE, D_LAT), D_NOPE ** -0.5, 0.5, ((0, 16),))
    w_uv = centred(seeds[5], (HEADS, D_LAT, D_V), D_LAT ** -0.5, 0.25, ((0, 16),))
    attn_out = centred(seeds[6], (TOKENS, HEADS * D_V), 1.0, 6.0, ((0, 32), (1, 16)))
    d_out = centred(seeds[7], (TOKENS, HEADS * D_V), 1.0, 6.0, ((0, 32), (1, 16)))
    span_table = draw_span_table(jax.random.fold_in(seeds[9], 71), 0)
    return dict(q_nope=q_nope, q_rope=q_rope, kv_cache=kv_cache, kv_gain=kv_gain, w_uk=w_uk, w_uv=w_uv, attn_out=attn_out, d_out=d_out, span_table=span_table)


eps_norm = 1e-06

def rounded(values):
    return lax.optimization_barrier(values.astype(jnp.bfloat16)).astype(jnp.float32)

def reference(q_nope, q_rope, kv_cache, kv_gain, w_uk, w_uv, attn_out, d_out, span_table):
    score_scale = float(D_NOPE + D_ROPE) ** (-0.5)
    head_group = HEADS // N_HEAD
    gain_rows = kv_gain.astype(jnp.float32)
    raw_rows = kv_cache[:, :D_LAT].astype(jnp.float32)
    inverse = lax.rsqrt(lax.optimization_barrier(jnp.mean(raw_rows * raw_rows, axis=1, keepdims=True)) + eps_norm)
    latent = (raw_rows * inverse * gain_rows).astype(jnp.bfloat16)
    key_cat = jnp.concatenate([latent, kv_cache[:, D_LAT:]], axis=1).astype(jnp.float32)
    key_lat = key_cat[:, :D_LAT]
    row_ids = jnp.arange(TOKENS, dtype=jnp.int32)
    positions = (span_table.reshape(-1)[row_ids // SPAN] * SPAN + row_ids % SPAN).astype(jnp.int32)
    w_uk_wide = w_uk.astype(jnp.float32)
    nope_rows = q_nope.reshape(TOKENS, HEADS, D_NOPE).astype(jnp.float32)
    q_latent = jnp.einsum('thn,hnl->thl', nope_rows, w_uk_wide).astype(jnp.bfloat16)
    queries = jnp.concatenate([q_latent, q_rope.reshape(TOKENS, HEADS, D_ROPE)], axis=2)
    grad_rows = d_out.reshape(TOKENS, HEADS, D_V).astype(jnp.float32)
    d_latent = jnp.einsum('thv,hlv->thl', grad_rows, w_uv.astype(jnp.float32)).astype(jnp.bfloat16)
    row_delta = lax.optimization_barrier(jnp.sum(grad_rows * attn_out.reshape(TOKENS, HEADS, D_V).astype(jnp.float32), axis=2))

    def source(key_total, source_index):
        row_start = source_index * TOK_DEV
        query_rows = lax.dynamic_slice_in_dim(queries, row_start, TOK_DEV, 0).astype(jnp.float32)
        latent_grads = lax.dynamic_slice_in_dim(d_latent, row_start, TOK_DEV, 0).astype(jnp.float32)
        delta_rows = lax.dynamic_slice_in_dim(row_delta, row_start, TOK_DEV, 0)
        query_pos = lax.dynamic_slice_in_dim(positions, row_start, TOK_DEV, 0)
        scores = jnp.einsum('thd,kd->htk', query_rows, key_cat) * score_scale
        visible = positions[None, None, :] <= query_pos[None, :, None]
        scores = jnp.where(visible, scores, -jnp.inf)
        row_top = lax.optimization_barrier(jnp.max(scores, axis=2, keepdims=True))
        log_total = row_top + jnp.log(lax.optimization_barrier(jnp.sum(jnp.exp(scores - row_top), axis=2, keepdims=True)))
        attn_prob = jnp.exp(scores - log_total)
        prob_round = rounded(attn_prob)
        d_prob = jnp.einsum('thl,kl->htk', latent_grads, key_lat)
        d_score = rounded(attn_prob * (d_prob - jnp.transpose(delta_rows)[:, :, None]) * score_scale)
        d_query = jnp.einsum('htk,kd->thd', d_score, key_cat)
        group_score = d_score.reshape(N_HEAD, head_group, TOK_DEV, TOKENS)
        group_prob = prob_round.reshape(N_HEAD, head_group, TOK_DEV, TOKENS)
        group_query = query_rows.reshape(TOK_DEV, N_HEAD, head_group, D_LAT + D_ROPE)
        group_grad = latent_grads.reshape(TOK_DEV, N_HEAD, head_group, D_LAT)
        key_part = jnp.einsum('ghtk,tghd->gkd', group_score, group_query)
        prob_part = jnp.einsum('ghtk,tghl->gkl', group_prob, group_grad)
        key_part = jnp.concatenate([key_part[:, :, :D_LAT] + prob_part, key_part[:, :, D_LAT:]], axis=2)
        key_total = key_total + lax.optimization_barrier(jnp.sum(rounded(key_part), axis=0))
        d_nope = jnp.einsum('thl,hnl->thn', rounded(d_query[:, :, :D_LAT]), w_uk_wide).astype(jnp.bfloat16)
        d_rope = d_query[:, :, D_LAT:].astype(jnp.bfloat16)
        return (key_total, (d_nope, d_rope))
    start_total = jnp.zeros((TOKENS, D_LAT + D_ROPE), jnp.float32)
    key_total, (d_nope, d_rope) = lax.scan(source, start_total, jnp.arange(N_CTX, dtype=jnp.int32))
    scaled = key_total[:, :D_LAT] * gain_rows
    inner_mean = lax.optimization_barrier(jnp.mean(raw_rows * scaled, axis=1, keepdims=True))
    d_raw = inverse * scaled - raw_rows * inverse * inverse * inverse * inner_mean
    d_cache = jnp.concatenate([d_raw, key_total[:, D_LAT:]], axis=1)
    return (d_nope.reshape(TOKENS, HEADS * D_NOPE), d_rope.reshape(TOKENS, HEADS * D_ROPE), d_cache)
```

```python
import functools

import jax
import jax.numpy as jnp
from jax import lax
from jax.experimental import pallas as pl
from jax.experimental.pallas import tpu as pltpu
from jax.sharding import PartitionSpec as P

MESH = pl.DeviceIdType.MESH
NEG_BIG = -1e30
EPS_NORM = 1e-06
LOG2_E = 1.4426950408889634

NZ = 16
HALF = NZ // 2
NP = 4
PIECE = 16
SPAN = 64
HEADS = 4
ROWS = SPAN * HEADS
LAT = 512
ROPE = 64
CAT = LAT + ROPE
NOPE = 128
CHUNK = 256
FIRST = 8
OTHER = 9
BLANK = 4 * OTHER

f32 = jnp.float32
bf16 = jnp.bfloat16


def dot(a, b, ca, cb):
    return lax.dot_general(a, b, (((ca,), (cb,)), ((), ())), preferred_element_type=f32)


def wrap(value, size):
    return lax.rem(value + 2 * size, size)


def kernel(
    q_nope, q_rope, kv, gain, w_uk, w_uv, attn_out, d_out, table,
    dq_nope_out, dq_rope_out, d_cache_out,
    keys, terms, sib_in, line_mid, line_in, ring_in, cross, final, result,
    queries, d_latent, delta, scores, d_prob, tops, other_terms, dq_prefix, dq_first,
    stats, sums, acc, inverse,
    sib0_s, sib0_r, gz_s, gz_r, gp_s, gp_r, gs_s, gs_r,
    ra_s, ra_r, rb_s, rb_r, rz_s, rz_r, rx_s, rx_r, rf_s, rf_r, rl_s, rl_r,
):
    scale = float(NOPE + ROPE) ** (-0.5)
    ctx = lax.axis_index("ctx")
    head = lax.axis_index("head")
    z, core = lax.div(ctx, 2), lax.rem(ctx, 2)
    x, y = lax.div(head, NP), lax.rem(head, NP)
    p = y * (1 - core) + x * core
    o = x * (1 - core) + y * core
    twin = 1 - core

    def at_own(pp):
        return {"ctx": ctx, "head": (1 - core) * (x * NP + pp) + core * (pp * NP + y)}

    def at_other(oo):
        return {"ctx": ctx, "head": (1 - core) * (oo * NP + y) + core * (x * NP + oo)}

    def at_z(zz):
        return {"ctx": zz * 2 + core, "head": head}

    sibling = {"ctx": z * 2 + twin, "head": head}
    right, left, far = wrap(p + 1, NP), wrap(p - 1, NP), wrap(p + 2, NP)
    up, down = wrap(z + 1, NZ), wrap(z - 1, NZ)

    def remote(src, dst, send, recv, device):
        return pltpu.make_async_remote_copy(
            src_ref=src, dst_ref=dst, send_sem=send, recv_sem=recv,
            device_id=device, device_id_type=MESH,
        )

    barrier = pltpu.get_barrier_semaphore()
    peers = [sibling, at_z(up), at_z(down)]
    peers += [at_own(wrap(p + j, NP)) for j in (1, 2, 3)]
    peers += [at_other(wrap(o + j, NP)) for j in (1, 2, 3)]
    for peer in peers:
        pl.semaphore_signal(barrier, inc=1, device_id=peer, device_id_type=MESH)

    raw = kv[:, :LAT].astype(f32)
    inv_norm = lax.rsqrt(jnp.mean(raw * raw, axis=-1, keepdims=True) + EPS_NORM)
    latent = (raw * inv_norm * gain[...].astype(f32)).astype(bf16)
    own_rope = kv[:, LAT:]
    for half in range(2):
        for pp in range(NP):
            rows = slice((half * NP + pp) * PIECE, (half * NP + pp + 1) * PIECE)
            keys[half, z, pp, core, :, :LAT] = latent[rows]
            keys[half, z, pp, core, :, LAT:] = own_rope[rows]

    pl.semaphore_wait(barrier, len(peers))
    first_copy = remote(
        keys.at[:, z, :, core], keys.at[:, z, :, core], sib0_s.at[0], sib0_r.at[0], sibling
    )
    first_copy.start()

    for h in range(HEADS):
        cols = slice(h * NOPE, (h + 1) * NOPE)
        rows = slice(h * SPAN, (h + 1) * SPAN)
        q_lat = dot(q_nope[:, cols], w_uk[h], 1, 0).astype(bf16)
        d_lat = dot(d_out[:, cols], w_uv[h], 1, 1).astype(bf16)
        for half in range(2):
            toks = slice(half * SPAN, (half + 1) * SPAN)
            queries[half, rows, :LAT] = q_lat[toks]
            queries[half, rows, LAT:] = q_rope[toks, h * ROPE : (h + 1) * ROPE]
            d_latent[half, rows, :] = d_lat[toks]
    for half in range(2):
        toks = slice(half * SPAN, (half + 1) * SPAN)
        prods = [
            d_out[toks, h * NOPE : (h + 1) * NOPE].astype(f32)
            * attn_out[toks, h * NOPE : (h + 1) * NOPE].astype(f32)
            for h in range(HEADS)
        ]
        prod = jnp.concatenate(prods, axis=0)
        delta[half] = jnp.sum(prod.T, axis=0, keepdims=True)

    def invert(b, carry):
        found = jnp.int32(0)
        for d in range(2 * NZ):
            found = found + jnp.where(table[d, 0] == b, d, 0)
        inverse[b] = jnp.minimum(found, 2 * NZ - 1)
        return carry

    lax.fori_loop(0, 2 * NZ, invert, 0)
    mine = table[ctx, 0]
    low_chunks = lax.div(mine + 4, 4)

    tops[...] = jnp.full(tops.shape, NEG_BIG, f32)
    dq_first[...] = jnp.zeros(dq_first.shape, f32)
    other_terms[BLANK] = jnp.zeros((SPAN, CAT), f32)

    first_copy.wait()

    def g_unit(ty, t):
        return wrap(z - t, NZ) if ty == 0 else wrap(z + t, NZ)

    g_last = (HALF, HALF - 1)

    def gz(ty, t):
        ref = keys.at[core, g_unit(ty, t), p]
        device = at_z(up) if ty == 0 else at_z(down)
        return remote(ref, ref, gz_s.at[ty, t], gz_r.at[ty, t], device)

    def gz_arrival(ty, t):
        ref = keys.at[core, g_unit(ty, t), p]
        device = at_z(up) if ty == 0 else at_z(down)
        return remote(ref, ref, gz_s.at[ty, t - 1], gz_r.at[ty, t - 1], device)

    def gp(ty, t, slot, piece, device):
        ref = keys.at[core, g_unit(ty, t), piece]
        return remote(ref, ref, gp_s.at[ty, t, slot], gp_r.at[ty, t, slot], device)

    def gs(ty, t, which):
        ref = keys.at[which, g_unit(ty, t)]
        return remote(ref, ref, gs_s.at[ty, t], gs_r.at[ty, t], sibling)

    def first_keys(t):
        low = keys[0, wrap(z - t, NZ)].reshape(CHUNK // 2, CAT)
        high = keys[0, wrap(z + lax.rem(t, HALF), NZ)].reshape(CHUNK // 2, CAT)
        return jnp.concatenate([low, high], axis=0)

    def fold_rows(value, op):
        part = value[0:8]
        for r in range(8, value.shape[0], 8):
            part = op(part, value[r : r + 8])
        return part

    def gather_step(t, carry):
        for ty in range(2):
            last = g_last[ty]

            @pl.when((t >= 1) & (t <= last))
            def _():
                gz_arrival(ty, t).wait_recv()

            @pl.when(t < last)
            def _():
                gz(ty, t).start()

            @pl.when((t >= 1) & (t <= last))
            def _():
                gp(ty, t, 0, p, at_own(right)).start()
                gp(ty, t, 1, p, at_own(left)).start()

        for ty in range(2):
            last = g_last[ty]

            @pl.when((t - 1 >= 1) & (t - 1 <= last))
            def _():
                tt = t - 1
                if ty == 0:
                    gp(ty, tt, 0, left, at_own(right)).wait_recv()
                    gp(ty, tt, 2, left, at_own(right)).start()
                    gp(ty, tt, 1, right, at_own(left)).wait_recv()
                else:
                    gp(ty, tt, 1, right, at_own(left)).wait_recv()
                    gp(ty, tt, 2, right, at_own(left)).start()
                    gp(ty, tt, 0, left, at_own(right)).wait_recv()

        for ty in range(2):
            last = g_last[ty]

            @pl.when((t - 2 >= 1) & (t - 2 <= last))
            def _():
                tt = t - 2
                gp(ty, tt, 2, far, at_own(right)).wait_recv()
                gs(ty, tt, core).start()

        for ty in range(2):
            last = g_last[ty]

            @pl.when((t - 3 >= 1) & (t - 3 <= last))
            def _():
                gs(ty, t - 3, twin).wait_recv()

        @pl.when(t - 3 >= 1)
        def _():
            tt = t - 3
            chunk = first_keys(tt)
            part = dot(chunk, queries[1], 1, 1)
            scores[tt - 1] = part
            tops[OTHER] = jnp.maximum(tops[OTHER], fold_rows(part, jnp.maximum))
            d_prob[tt - 1] = dot(chunk[:, :LAT], d_latent[1], 1, 1)

        return carry

    lax.fori_loop(0, HALF + 4, gather_step, 0)

    def kind_of(j):
        return jnp.where(j >= low_chunks, 1, 0)

    def other_keys(j):
        kind = kind_of(j)
        blocks = []
        for i in range(4):
            low_id = inverse[jnp.minimum(4 * j + i, 2 * NZ - 1)]
            high_id = inverse[jnp.clip(2 * NZ - 1 - (4 * (j - low_chunks) + i), 0, 2 * NZ - 1)]
            owner = jnp.where(kind == 1, high_id, low_id)
            block = keys[kind, lax.div(owner, 2), :, lax.rem(owner, 2)]
            blocks.append(block.reshape(SPAN, CAT))
        return jnp.concatenate(blocks, axis=0)

    key_in = lax.broadcasted_iota(jnp.int32, (CHUNK, ROWS), 0)
    tok_in = lax.rem(lax.broadcasted_iota(jnp.int32, (CHUNK, ROWS), 1), SPAN)

    def other_scores(j, carry):
        kind = kind_of(j)
        chunk = other_keys(j)
        low_gap = (4 * j - mine) * SPAN
        high_gap = (4 * (j - low_chunks) - (2 * NZ - 1 - mine)) * SPAN
        gap = jnp.where(kind == 1, high_gap, low_gap)
        part = dot(chunk, queries[kind], 1, 1)
        part = jnp.where(key_in + gap <= tok_in, part, NEG_BIG)
        scores[FIRST + j] = part
        tops[j] = fold_rows(part, jnp.maximum)
        d_prob[FIRST + j] = dot(chunk[:, :LAT], d_latent[kind], 1, 1)
        return carry

    lax.fori_loop(0, OTHER, other_scores, 0)

    top_low = jnp.full((8, ROWS), NEG_BIG, f32)
    top_high = tops[OTHER]
    for j in range(OTHER):
        high = j >= low_chunks
        top_low = jnp.maximum(top_low, jnp.where(high, NEG_BIG, tops[j]))
        top_high = jnp.maximum(top_high, jnp.where(high, tops[j], NEG_BIG))
    rate = scale * LOG2_E
    stats[0] = jnp.max(top_low, axis=0, keepdims=True) * rate
    stats[1] = jnp.max(top_high, axis=0, keepdims=True) * rate

    def exponents(n, carry):
        kind = jnp.where(n < FIRST, 1, kind_of(n - FIRST))
        part = jnp.exp2(scores[n] * rate - stats[kind])
        scores[n] = part
        sums[n] = fold_rows(part, jnp.add)
        return carry

    lax.fori_loop(0, FIRST + OTHER, exponents, 0)

    sum_low = jnp.zeros((8, ROWS), f32)
    sum_high = jnp.zeros((8, ROWS), f32)
    for n in range(FIRST):
        sum_high = sum_high + sums[n]
    for j in range(OTHER):
        high = j >= low_chunks
        sum_low = sum_low + jnp.where(high, 0.0, sums[FIRST + j])
        sum_high = sum_high + jnp.where(high, sums[FIRST + j], 0.0)
    stats[0] = 1.0 / jnp.sum(sum_low, axis=0, keepdims=True)
    stats[1] = 1.0 / jnp.sum(sum_high, axis=0, keepdims=True)

    def chunk_grads(n, kind, chunk):
        expo = scores[n]
        inv_sum = stats[kind]
        prob = (expo * inv_sum).astype(bf16)
        d_score = ((d_prob[n] - delta[kind]) * (expo * (inv_sum * scale))).astype(bf16)
        dq = dot(d_score, chunk, 0, 0)
        dk = dot(d_score, queries[kind], 1, 0)
        dk_lat = dk[:, :LAT] + dot(prob, d_latent[kind], 1, 0)
        return dq, dk_lat, dk[:, LAT:]

    def other_grads(j, carry):
        dq, dk_lat, dk_rope = chunk_grads(FIRST + j, kind_of(j), other_keys(j))
        for i in range(4):
            rows = slice(i * SPAN, (i + 1) * SPAN)
            other_terms[4 * j + i, :, :LAT] = dk_lat[rows]
            other_terms[4 * j + i, :, LAT:] = dk_rope[rows]

        fresh = (j == 0) | (j == low_chunks)
        before = dq_prefix[jnp.maximum(j - 1, 0)]
        dq_prefix[j] = dq + jnp.where(fresh, 0.0, before)
        return carry

    dq_prefix[0] = jnp.zeros((ROWS, CAT), f32)
    lax.fori_loop(0, OTHER, other_grads, 0)

    def r_unit(ty, k):
        return wrap(z + k, NZ) if ty == 0 else wrap(z - k, NZ)

    r_first = (HALF, HALF - 1)
    r_end = (0, 1)

    def ra(ty, k):
        unit = r_unit(ty, k)
        return remote(terms.at[twin, unit], sib_in.at[unit], ra_s.at[ty, k], ra_r.at[ty, k], sibling)

    def rb(ty, k, slot, piece, dst, device):
        unit = r_unit(ty, k)
        return remote(
            terms.at[core, unit, piece], dst, rb_s.at[ty, k, slot], rb_r.at[ty, k, slot], device
        )

    def rb_mid(ty, k):
        unit = r_unit(ty, k)
        device = at_own(right) if ty == 0 else at_own(left)
        return rb(ty, k, 0, far, line_mid.at[unit], device)

    def rb_right(ty, k):
        return rb(ty, k, 1, right, line_in.at[r_unit(ty, k), 0], at_own(right))

    def rb_left(ty, k):
        return rb(ty, k, 2, left, line_in.at[r_unit(ty, k), 1], at_own(left))

    def rz(ty, k):
        unit = r_unit(ty, k)
        device = at_z(up) if ty == 0 else at_z(down)
        return remote(
            terms.at[core, unit, p], ring_in.at[ty, unit], rz_s.at[ty, k], rz_r.at[ty, k], device
        )

    def rz_arrival(ty, k, unit):
        device = at_z(up) if ty == 0 else at_z(down)
        return remote(
            terms.at[core, unit, p], ring_in.at[ty, unit],
            rz_s.at[ty, k + 1], rz_r.at[ty, k + 1], device,
        )

    def valid(ty, k):
        return (k >= r_end[ty]) & (k <= r_first[ty])

    def first_grads(k):
        n = k - 1
        dq, dk_lat, dk_rope = chunk_grads(n, 1, first_keys(k))
        dq_first[...] += dq
        units = (wrap(z - k, NZ), wrap(z + lax.rem(k, HALF), NZ))
        for s in range(2):
            unit = units[s]
            for cc in range(2):
                block = table[unit * 2 + cc, 0]
                low_slot = jnp.where(block < 4 * low_chunks, block, BLANK)
                high_slot = jnp.minimum(4 * low_chunks + (2 * NZ - 1 - block), BLANK)
                low_term = other_terms[low_slot]
                high_term = other_terms[high_slot].astype(bf16)
                for pp in range(NP):
                    src = slice(s * 128 + (pp * 2 + cc) * PIECE, s * 128 + (pp * 2 + cc + 1) * PIECE)
                    rows = slice(pp * PIECE, (pp + 1) * PIECE)
                    terms[0, unit, pp, cc, :, :LAT] = (
                        dk_lat[src] + low_term[rows, :LAT]
                    ).astype(bf16)
                    terms[0, unit, pp, cc, :, LAT:] = (
                        dk_rope[src] + low_term[rows, LAT:]
                    ).astype(bf16)
                    terms[1, unit, pp, cc] = high_term[rows]

    def query_outputs():
        low = dq_prefix[low_chunks - 1]
        high = dq_prefix[OTHER - 1] + dq_first[...]
        for half, part in ((0, low), (1, high)):
            toks = slice(half * SPAN, (half + 1) * SPAN)
            dq_lat = part[:, :LAT].astype(bf16)
            dq_rope = part[:, LAT:]
            for h in range(HEADS):
                rows = slice(h * SPAN, (h + 1) * SPAN)
                dq_nope_out[toks, h * NOPE : (h + 1) * NOPE] = dot(
                    dq_lat[rows], w_uk[h], 1, 1
                ).astype(bf16)
            for h in range(0, HEADS, 2):
                pair = jnp.concatenate(
                    [
                        dq_rope[h * SPAN : (h + 1) * SPAN],
                        dq_rope[(h + 1) * SPAN : (h + 2) * SPAN],
                    ],
                    axis=1,
                )
                dq_rope_out[toks, h * ROPE : (h + 2) * ROPE] = pair.astype(bf16)

    def reduce_step(i, carry):
        @pl.when(i < HALF)
        def _():
            first_grads(HALF - i)

        k = HALF - i
        for ty in range(2):

            @pl.when(valid(ty, k))
            def _():
                ra(ty, k).start()

        for ty in range(2):
            ka = k + 1

            @pl.when(valid(ty, ka))
            def _():
                unit = r_unit(ty, ka)
                ra(ty, ka).wait_recv()
                both = terms[core, unit].astype(f32) + sib_in[unit].astype(f32)
                terms[core, unit] = both.astype(bf16)
                rb_mid(ty, ka).start()

        for ty in range(2):
            kb = k + 2

            @pl.when(valid(ty, kb))
            def _():
                unit = r_unit(ty, kb)
                rb_mid(ty, kb).wait_recv()
                piece = right if ty == 0 else left
                both = terms[core, unit, piece].astype(f32) + line_mid[unit].astype(f32)
                terms[core, unit, piece] = both.astype(bf16)
                rb_right(ty, kb).start()
                rb_left(ty, kb).start()

        for ty in range(2):
            kc = k + 3

            @pl.when(valid(ty, kc))
            def _():
                unit = r_unit(ty, kc)
                rb_right(ty, kc).wait_recv()
                rb_left(ty, kc).wait_recv()
                acc[...] = (
                    terms[core, unit, p].astype(f32)
                    + line_in[unit, 0].astype(f32)
                    + line_in[unit, 1].astype(f32)
                )

                @pl.when(kc < r_first[ty])
                def _():
                    rz_arrival(ty, kc, unit).wait_recv()
                    acc[...] += ring_in[ty, unit].astype(f32)

                if ty == 0:

                    @pl.when(kc == 0)
                    def _():
                        rz_arrival(1, 0, unit).wait_recv()
                        acc[...] += ring_in[1, unit].astype(f32)

                terms[core, unit, p] = acc[...].astype(bf16)

                @pl.when(kc >= 1)
                def _():
                    rz(ty, kc).start()

        @pl.when(i == HALF)
        def _():
            query_outputs()

        return carry

    lax.fori_loop(0, HALF + 4, reduce_step, 0)

    cross[o] = terms[core, z, p]

    def rx(j, slot):
        return remote(
            cross.at[slot], cross.at[slot], rx_s.at[j], rx_r.at[j], at_other(wrap(o + j, NP))
        )

    for j in (1, 2, 3):
        rx(j, o).start()
    for j in (1, 2, 3):
        rx(j, wrap(o - j, NP)).wait_recv()
    total = cross[0].astype(f32)
    for j in (1, 2, 3):
        total = total + cross[j].astype(f32)
    final[p] = total.astype(bf16)

    def rf(j, slot):
        return remote(
            final.at[slot], final.at[slot], rf_s.at[j], rf_r.at[j], at_own(wrap(p + j, NP))
        )

    for j in (1, 2, 3):
        rf(j, p).start()
    for j in (1, 2, 3):
        rf(j, wrap(p - j, NP)).wait_recv()

    def rl(which, half):
        return remote(final.at[:, which], result.at[half], rl_s.at[0], rl_r.at[0], sibling)

    rl(twin, core).start()
    result[core] = final[:, core]
    rl(core, twin).wait_recv()

    gain_row = gain[...].astype(f32)
    for half in range(2):
        toks = slice(half * SPAN, (half + 1) * SPAN)
        grads = result[half].reshape(SPAN, CAT).astype(f32)
        values = kv[toks, :LAT].astype(f32)
        inv = lax.rsqrt(jnp.mean(values * values, axis=-1, keepdims=True) + EPS_NORM)
        scaled = grads[:, :LAT] * gain_row
        inner = jnp.mean(values * scaled, axis=-1, keepdims=True)
        d_cache_out[toks, :LAT] = inv * scaled - values * (inv * inv * inv * inner)
        d_cache_out[toks, LAT:] = grads[:, LAT:]

    def gather_sends(t, carry):
        for ty in range(2):

            @pl.when(t < g_last[ty])
            def _():
                gz(ty, t).wait_send()

            @pl.when((t >= 1) & (t <= g_last[ty]))
            def _():
                gp(ty, t, 0, p, at_own(right)).wait_send()
                gp(ty, t, 1, p, at_own(left)).wait_send()
                if ty == 0:
                    gp(ty, t, 2, left, at_own(right)).wait_send()
                else:
                    gp(ty, t, 2, right, at_own(left)).wait_send()
                gs(ty, t, core).wait_send()

        return carry

    lax.fori_loop(0, HALF + 1, gather_sends, 0)

    def reduce_sends(k, carry):
        for ty in range(2):

            @pl.when(valid(ty, k))
            def _():
                ra(ty, k).wait_send()
                rb_mid(ty, k).wait_send()
                rb_right(ty, k).wait_send()
                rb_left(ty, k).wait_send()

                @pl.when(k >= 1)
                def _():
                    rz(ty, k).wait_send()

        return carry

    lax.fori_loop(0, HALF + 1, reduce_sends, 0)
    for j in (1, 2, 3):
        rx(j, o).wait_send()
        rf(j, p).wait_send()
    rl(twin, core).wait_send()


def local(q_nope, q_rope, kv_cache, kv_gain, w_uk, w_uv, attn_out, d_out, span_table):
    toks = q_nope.shape[0]
    vmem = pl.BlockSpec(memory_space=pltpu.VMEM)
    smem = pl.BlockSpec(memory_space=pltpu.SMEM)
    dma = pltpu.SemaphoreType.DMA
    scratch = [
        pltpu.VMEM((2, NZ, NP, 2, PIECE, CAT), bf16),
        pltpu.VMEM((2, NZ, NP, 2, PIECE, CAT), bf16),
        pltpu.VMEM((NZ, NP, 2, PIECE, CAT), bf16),
        pltpu.VMEM((NZ, 2, PIECE, CAT), bf16),
        pltpu.VMEM((NZ, 2, 2, PIECE, CAT), bf16),
        pltpu.VMEM((2, NZ, 2, PIECE, CAT), bf16),
        pltpu.VMEM((NP, 2, PIECE, CAT), bf16),
        pltpu.VMEM((NP, 2, PIECE, CAT), bf16),
        pltpu.VMEM((2, NP, PIECE, CAT), bf16),
        pltpu.VMEM((2, ROWS, CAT), bf16),
        pltpu.VMEM((2, ROWS, LAT), bf16),
        pltpu.VMEM((2, 1, ROWS), f32),
        pltpu.VMEM((FIRST + OTHER, CHUNK, ROWS), f32),
        pltpu.VMEM((FIRST + OTHER, CHUNK, ROWS), f32),
        pltpu.VMEM((OTHER + 1, 8, ROWS), f32),
        pltpu.VMEM((BLANK + 1, SPAN, CAT), f32),
        pltpu.VMEM((OTHER, ROWS, CAT), f32),
        pltpu.VMEM((ROWS, CAT), f32),
        pltpu.VMEM((2, 1, ROWS), f32),
        pltpu.VMEM((FIRST + OTHER, 8, ROWS), f32),
        pltpu.VMEM((2, PIECE, CAT), f32),
        pltpu.SMEM((2 * NZ,), jnp.int32),
        dma((1,)), dma((1,)),
        dma((2, HALF + 1)), dma((2, HALF + 1)),
        dma((2, HALF + 1, 3)), dma((2, HALF + 1, 3)),
        dma((2, HALF + 1)), dma((2, HALF + 1)),
        dma((2, HALF + 1)), dma((2, HALF + 1)),
        dma((2, HALF + 1, 3)), dma((2, HALF + 1, 3)),
        dma((2, HALF + 2)), dma((2, HALF + 2)),
        dma((NP,)), dma((NP,)),
        dma((NP,)), dma((NP,)),
        dma((1,)), dma((1,)),
    ]
    return pl.pallas_call(
        kernel,
        out_shape=(
            jax.ShapeDtypeStruct((toks, HEADS * NOPE), bf16),
            jax.ShapeDtypeStruct((toks, HEADS * ROPE), bf16),
            jax.ShapeDtypeStruct((toks, CAT), f32),
        ),
        in_specs=[vmem] * 8 + [smem],
        out_specs=(vmem, vmem, vmem),
        scratch_shapes=scratch,
        compiler_params=pltpu.CompilerParams(
            collective_id=0, has_side_effects=True, vmem_limit_bytes=56 * 1024 * 1024
        ),
    )(q_nope, q_rope, kv_cache, kv_gain.reshape(1, LAT), w_uk, w_uv, attn_out, d_out, span_table)


def solution(mesh):
    in_specs = (
        P("ctx", "head"),
        P("ctx", "head"),
        P("ctx", None),
        P(),
        P("head", None, None),
        P("head", None, None),
        P("ctx", "head"),
        P("ctx", "head"),
        P(),
    )
    out_specs = (P("ctx", "head"), P("ctx", "head"), P("ctx", None))
    return jax.shard_map(local, mesh=mesh, in_specs=in_specs, out_specs=out_specs, check_vma=False)
```

```python
import functools

import jax
import jax.numpy as jnp
from jax import lax
from jax.experimental import pallas as pl
from jax.experimental.pallas import tpu as pltpu
from jax.sharding import PartitionSpec as P

MESH = pl.DeviceIdType.MESH
NEG_BIG = -1e30
EPS_NORM = 1e-06
LOG2_E = 1.4426950408889634

NZ = 16
HALF = NZ // 2
NP = 4
PIECE = 16
SPAN = 64
HEADS = 4
ROWS = SPAN * HEADS
LAT = 512
ROPE = 64
CAT = LAT + ROPE
NOPE = 128
CHUNK = 256
FIRST = 8
OTHER = 9
BLANK = 4 * OTHER

f32 = jnp.float32
bf16 = jnp.bfloat16


def dot(a, b, ca, cb):
    return lax.dot_general(a, b, (((ca,), (cb,)), ((), ())), preferred_element_type=f32)


def wrap(value, size):
    return lax.rem(value + 2 * size, size)


def kernel(
    q_nope_in, q_rope_in, kv_in, gain_in, w_uk_in, w_uv_in, attn_out_in, d_out_in, table,
    dq_nope_res, dq_rope_res, d_cache_res,
    q_nope, q_rope, kv_t, gain, w_uk, w_uv, attn_out, d_out,
    dq_nope_out, dq_rope_out, d_cache_out,
    keys, terms, sib_in, line_in, piece_in, ring_in, share, share_in, final, result,
    queries, d_latent, delta, scores, d_prob, tops, other_terms, dq_prefix, dq_first,
    stats, sums, inverse, in_sem, out_sem,
    g0_s, g0_r, gz_s, gz_r, gp_s, gp_r, gl_s, gl_r, gs_s, gs_r,
    ra_s, ra_r, rl_s, rl_r, rp_s, rp_r, rz_s, rz_r, rh_s, rh_r, f1_s, f1_r, f2_s, f2_r,
):
    scale = float(NOPE + ROPE) ** (-0.5)
    ctx = lax.axis_index("ctx")
    head = lax.axis_index("head")
    z, core = lax.div(ctx, 2), lax.rem(ctx, 2)
    x, y = lax.div(head, NP), lax.rem(head, NP)
    twin = 1 - core

    def at_x(j):
        return {"ctx": ctx, "head": wrap(x + j, NP) * NP + y}

    def at_y(j):
        return {"ctx": ctx, "head": x * NP + wrap(y + j, NP)}

    def at_z(zz):
        return {"ctx": zz * 2 + core, "head": head}

    sibling = {"ctx": z * 2 + twin, "head": head}

    def remote(src, dst, send, recv, device):
        return pltpu.make_async_remote_copy(
            src_ref=src, dst_ref=dst, send_sem=send, recv_sem=recv,
            device_id=device, device_id_type=MESH,
        )

    def by_core(step):
        for c in range(2):
            pl.when(core == c)(functools.partial(step, c))

    barrier = pltpu.get_barrier_semaphore()
    peers = [at_z(wrap(z + d, NZ)) for d in (8, 7, 9, 6, 10, 5, 11, 4, 12, 3, 13, 2, 14, 1, 15)]
    peers += [at_x(j) for j in (1, 2, 3)] + [at_y(j) for j in (1, 2, 3)] + [sibling]
    for peer in peers:
        pl.semaphore_signal(barrier, inc=1, device_id=peer, device_id_type=MESH)

    loads = [
        pltpu.make_async_copy(src, dst, in_sem.at[n])
        for n, (src, dst) in enumerate(
            (
                (kv_in, kv_t), (gain_in, gain), (q_nope_in, q_nope), (w_uk_in, w_uk),
                (q_rope_in, q_rope), (d_out_in, d_out), (w_uv_in, w_uv), (attn_out_in, attn_out),
            )
        )
    ]
    for load in loads:
        load.start()

    loads[0].wait()
    loads[1].wait()
    kv = kv_t[...].T
    raw = kv[:, :LAT].astype(f32)
    inv_norm = lax.rsqrt(jnp.mean(raw * raw, axis=-1, keepdims=True) + EPS_NORM)
    latent = (raw * inv_norm * gain[...].astype(f32)).astype(bf16)
    own_rope = kv[:, LAT:]
    for half in range(2):
        rows = slice(half * SPAN, (half + 1) * SPAN)
        keys[z, 2 * half + core, :, :, :LAT] = latent[rows].reshape(NP, PIECE, LAT)
        keys[z, 2 * half + core, :, :, LAT:] = own_rope[rows].reshape(NP, PIECE, ROPE)

    for load in loads[2:]:
        load.wait()
    for h in range(HEADS):
        cols = slice(h * NOPE, (h + 1) * NOPE)
        rows = slice(h * SPAN, (h + 1) * SPAN)
        q_lat = dot(q_nope[:, cols], w_uk[h], 1, 0).astype(bf16)
        d_lat = dot(d_out[:, cols], w_uv[h], 1, 1).astype(bf16)
        for half in range(2):
            toks = slice(half * SPAN, (half + 1) * SPAN)
            queries[half, rows, :LAT] = q_lat[toks]
            queries[half, rows, LAT:] = q_rope[toks, h * ROPE : (h + 1) * ROPE]
            d_latent[half, rows, :] = d_lat[toks]
    for half in range(2):
        toks = slice(half * SPAN, (half + 1) * SPAN)
        prods = [
            d_out[toks, h * NOPE : (h + 1) * NOPE].astype(f32)
            * attn_out[toks, h * NOPE : (h + 1) * NOPE].astype(f32)
            for h in range(HEADS)
        ]
        prod = jnp.concatenate(prods, axis=0)
        delta[half] = jnp.sum(prod.T, axis=0, keepdims=True)

    tops[...] = jnp.full(tops.shape, NEG_BIG, f32)
    dq_first[...] = jnp.zeros(dq_first.shape, f32)
    other_terms[BLANK] = jnp.zeros((SPAN, CAT), f32)

    pl.semaphore_wait(barrier, len(peers))

    def g_last(c):
        return HALF if c == 0 else HALF - 1

    def g_unit(c, d):
        return wrap(z - d, NZ) if c == 0 else wrap(z + d, NZ)

    def g_own(n):
        ref = keys.at[z, 2 * n + core]
        return remote(ref, ref, g0_s.at[n], g0_r.at[n], sibling)

    def g_own_arrival(n):
        ref = keys.at[z, 2 * n + twin]
        return remote(ref, ref, g0_s.at[n], g0_r.at[n], sibling)

    def gz(c, d, unit):
        ref = keys.at[unit, x, y]
        device = at_z(wrap(z + d, NZ) if c == 0 else wrap(z - d, NZ))
        return remote(ref, ref, gz_s.at[d], gz_r.at[d], device)

    def gp(c, d, j, back):
        unit = g_unit(c, d)
        if c == 0:
            ref, device = keys.at[unit, wrap(x - back, NP), y], at_x(j)
        else:
            ref, device = keys.at[unit, x, wrap(y - back, NP)], at_y(j)
        return remote(ref, ref, gp_s.at[d, j], gp_r.at[d, j], device)

    def gl(c, d, j, back):
        unit = g_unit(c, d)
        if c == 0:
            ref, device = keys.at[unit, :, wrap(y - back, NP)], at_y(j)
        else:
            ref, device = keys.at[unit, wrap(x - back, NP)], at_x(j)
        return remote(ref, ref, gl_s.at[d, j], gl_r.at[d, j], device)

    def gs(c, d):
        ref = keys.at[g_unit(c, d)]
        return remote(ref, ref, gs_s.at[d], gs_r.at[d], sibling)

    for n in range(2):
        g_own(n).start()
    for n in range(2):
        g_own_arrival(n).wait_recv()

    def each(low, high, step):
        def body(d, carry):
            step(d)
            return carry

        lax.fori_loop(low, high, body, 0)

    def spread_z(c):
        each(1, g_last(c) + 1, lambda d: gz(c, d, z).start())

    by_core(spread_z)

    def invert(b, carry):
        found = jnp.int32(0)
        for d in range(2 * NZ):
            found = found + jnp.where(table[0, d] == b, d, 0)
        inverse[b] = jnp.minimum(found, 2 * NZ - 1)
        return carry

    lax.fori_loop(0, 2 * NZ, invert, 0)
    mine = table[0, ctx]
    low_chunks = lax.div(mine + 4, 4)

    def spread_piece(c):
        def step(d):
            gz(c, d, g_unit(c, d)).wait_recv()
            for j in (2, 1, 3):
                gp(c, d, j, 0).start()

        each(1, g_last(c) + 1, step)

    by_core(spread_piece)

    def spread_line(c):
        def step(d):
            for j in (1, 2, 3):
                gp(c, d, j, j).wait_recv()
            for j in (2, 1, 3):
                gl(c, d, j, 0).start()

        each(1, g_last(c) + 1, step)

    by_core(spread_line)

    def first_keys(t):
        low = keys[wrap(z - t, NZ), 0:2].reshape(CHUNK // 2, CAT)
        high = keys[wrap(z + lax.rem(t, HALF), NZ), 0:2].reshape(CHUNK // 2, CAT)
        return jnp.concatenate([low, high], axis=0)

    def fold_rows(value, op):
        part = value[0:8]
        for r in range(8, value.shape[0], 8):
            part = op(part, value[r : r + 8])
        return part

    def arrivals(d):
        def own(c):
            @pl.when(d <= g_last(c))
            def _():
                for j in (1, 2, 3):
                    gl(c, d, j, j).wait_recv()
                gs(c, d).start()

            @pl.when((d >= 2) & (d - 1 <= g_last(1 - c)))
            def _():
                gs(1 - c, d - 1).wait_recv()

        by_core(own)

        @pl.when(d >= 2)
        def _():
            t = d - 1
            chunk = first_keys(t)
            part = dot(chunk, queries[1], 1, 1)
            scores[t - 1] = part
            tops[OTHER] = jnp.maximum(tops[OTHER], fold_rows(part, jnp.maximum))
            d_prob[t - 1] = dot(chunk[:, :LAT], d_latent[1], 1, 1)

    each(1, HALF + 2, arrivals)

    def kind_of(j):
        return jnp.where(j >= low_chunks, 1, 0)

    def other_keys(j):
        kind = kind_of(j)
        blocks = []
        for i in range(4):
            low_id = inverse[jnp.minimum(4 * j + i, 2 * NZ - 1)]
            high_id = inverse[jnp.clip(2 * NZ - 1 - (4 * (j - low_chunks) + i), 0, 2 * NZ - 1)]
            owner = jnp.where(kind == 1, high_id, low_id)
            block = keys[lax.div(owner, 2), 2 * kind + lax.rem(owner, 2)]
            blocks.append(block.reshape(SPAN, CAT))
        return jnp.concatenate(blocks, axis=0)

    key_in = lax.broadcasted_iota(jnp.int32, (CHUNK, ROWS), 0)
    tok_in = lax.rem(lax.broadcasted_iota(jnp.int32, (CHUNK, ROWS), 1), SPAN)

    def other_scores(j, carry):
        kind = kind_of(j)
        chunk = other_keys(j)
        low_gap = (4 * j - mine) * SPAN
        high_gap = (4 * (j - low_chunks) - (2 * NZ - 1 - mine)) * SPAN
        gap = jnp.where(kind == 1, high_gap, low_gap)
        part = dot(chunk, queries[kind], 1, 1)
        part = jnp.where(key_in + gap <= tok_in, part, NEG_BIG)
        scores[FIRST + j] = part
        tops[j] = fold_rows(part, jnp.maximum)
        d_prob[FIRST + j] = dot(chunk[:, :LAT], d_latent[kind], 1, 1)
        return carry

    lax.fori_loop(0, OTHER, other_scores, 0)

    top_low = jnp.full((8, ROWS), NEG_BIG, f32)
    top_high = tops[OTHER]
    for j in range(OTHER):
        high = j >= low_chunks
        top_low = jnp.maximum(top_low, jnp.where(high, NEG_BIG, tops[j]))
        top_high = jnp.maximum(top_high, jnp.where(high, tops[j], NEG_BIG))
    rate = scale * LOG2_E
    stats[0] = jnp.max(top_low, axis=0, keepdims=True) * rate
    stats[1] = jnp.max(top_high, axis=0, keepdims=True) * rate

    def exponents(n, carry):
        kind = jnp.where(n < FIRST, 1, kind_of(n - FIRST))
        part = jnp.exp2(scores[n] * rate - stats[kind])
        scores[n] = part
        sums[n] = fold_rows(part, jnp.add)
        return carry

    lax.fori_loop(0, FIRST + OTHER, exponents, 0)

    sum_low = jnp.zeros((8, ROWS), f32)
    sum_high = jnp.zeros((8, ROWS), f32)
    for n in range(FIRST):
        sum_high = sum_high + sums[n]
    for j in range(OTHER):
        high = j >= low_chunks
        sum_low = sum_low + jnp.where(high, 0.0, sums[FIRST + j])
        sum_high = sum_high + jnp.where(high, sums[FIRST + j], 0.0)
    stats[0] = 1.0 / jnp.sum(sum_low, axis=0, keepdims=True)
    stats[1] = 1.0 / jnp.sum(sum_high, axis=0, keepdims=True)

    def chunk_grads(n, kind, chunk):
        expo = scores[n]
        inv_sum = stats[kind]
        prob = (expo * inv_sum).astype(bf16)
        d_score = ((d_prob[n] - delta[kind]) * (expo * (inv_sum * scale))).astype(bf16)
        dq = dot(d_score, chunk, 0, 0)
        dk = dot(d_score, queries[kind], 1, 0)
        dk_lat = dk[:, :LAT] + dot(prob, d_latent[kind], 1, 0)
        return dq, dk_lat, dk[:, LAT:]

    def other_grads(j, carry):
        dq, dk_lat, dk_rope = chunk_grads(FIRST + j, kind_of(j), other_keys(j))
        for i in range(4):
            rows = slice(i * SPAN, (i + 1) * SPAN)
            other_terms[4 * j + i, :, :LAT] = dk_lat[rows]
            other_terms[4 * j + i, :, LAT:] = dk_rope[rows]

        fresh = (j == 0) | (j == low_chunks)
        before = dq_prefix[jnp.maximum(j - 1, 0)]
        dq_prefix[j] = dq + jnp.where(fresh, 0.0, before)
        return carry

    dq_prefix[0] = jnp.zeros((ROWS, CAT), f32)
    lax.fori_loop(0, OTHER, other_grads, 0)

    def r_first(c):
        return HALF if c == 0 else HALF - 1

    def r_end(c):
        return 1 if c == 0 else 0

    def r_unit(c, k):
        return wrap(z + k, NZ) if c == 0 else wrap(z - k, NZ)

    def ra(c, k):
        return remote(terms.at[r_unit(c, k)], sib_in.at[k], ra_s.at[k], ra_r.at[k], sibling)

    def rl(c, k, j):
        unit = r_unit(c, k)
        if c == 0:
            ref, device = terms.at[unit, :, wrap(y + j, NP)], at_y(j)
        else:
            ref, device = terms.at[unit, wrap(x + j, NP)], at_x(j)
        return remote(ref, line_in.at[k, j - 1], rl_s.at[k, j], rl_r.at[k, j], device)

    def rp(c, k, j):
        unit = r_unit(c, k)
        if c == 0:
            ref, device = terms.at[unit, wrap(x + j, NP), y], at_x(j)
        else:
            ref, device = terms.at[unit, x, wrap(y + j, NP)], at_y(j)
        return remote(ref, piece_in.at[k, j - 1], rp_s.at[k, j], rp_r.at[k, j], device)

    def rz(c, k):
        unit = r_unit(c, k)
        return remote(terms.at[unit, x, y], ring_in.at[k], rz_s.at[k], rz_r.at[k], at_z(unit))

    def first_grads(k):
        n = k - 1
        dq, dk_lat, dk_rope = chunk_grads(n, 1, first_keys(k))
        dq_first[...] += dq
        units = (wrap(z - k, NZ), wrap(z + lax.rem(k, HALF), NZ))
        for s in range(2):
            unit = units[s]
            for cc in range(2):
                block = table[0, unit * 2 + cc]
                low_slot = jnp.where(block < 4 * low_chunks, block, BLANK)
                high_slot = jnp.minimum(4 * low_chunks + (2 * NZ - 1 - block), BLANK)
                low_term = other_terms[low_slot]
                rows = slice((2 * s + cc) * SPAN, (2 * s + cc + 1) * SPAN)
                terms[unit, cc, :, :, :LAT] = (
                    (dk_lat[rows] + low_term[:, :LAT]).astype(bf16).reshape(NP, PIECE, LAT)
                )
                terms[unit, cc, :, :, LAT:] = (
                    (dk_rope[rows] + low_term[:, LAT:]).astype(bf16).reshape(NP, PIECE, ROPE)
                )
                terms[unit, 2 + cc] = other_terms[high_slot].astype(bf16).reshape(NP, PIECE, CAT)

    def reduce_step(i):
        @pl.when(i < HALF)
        def _():
            first_grads(HALF - i)

        k = HALF - i

        def own(c):
            @pl.when((k >= r_end(1 - c)) & (k <= r_first(1 - c)))
            def _():
                ra(1 - c, k).start()

            ka = k + 1

            @pl.when((ka >= r_end(c)) & (ka <= r_first(c)))
            def _():
                unit = r_unit(c, ka)
                ra(c, ka).wait_recv()
                both = terms[unit].astype(f32) + sib_in[ka].astype(f32)
                terms[unit] = both.astype(bf16)
                for j in (2, 1, 3):
                    rl(c, ka, j).start()

        by_core(own)

    each(0, HALF + 2, reduce_step)

    low = dq_prefix[low_chunks - 1]
    high = dq_prefix[OTHER - 1] + dq_first[...]
    for half, part in ((0, low), (1, high)):
        toks = slice(half * SPAN, (half + 1) * SPAN)
        dq_lat = part[:, :LAT].astype(bf16)
        dq_rope = part[:, LAT:]
        for h in range(HEADS):
            rows = slice(h * SPAN, (h + 1) * SPAN)
            dq_nope_out[toks, h * NOPE : (h + 1) * NOPE] = dot(
                dq_lat[rows], w_uk[h], 1, 1
            ).astype(bf16)
        for h in range(0, HEADS, 2):
            pair = jnp.concatenate(
                [dq_rope[h * SPAN : (h + 1) * SPAN], dq_rope[(h + 1) * SPAN : (h + 2) * SPAN]],
                axis=1,
            )
            dq_rope_out[toks, h * ROPE : (h + 2) * ROPE] = pair.astype(bf16)
    stores = [
        pltpu.make_async_copy(dq_nope_out, dq_nope_res, out_sem.at[0]),
        pltpu.make_async_copy(dq_rope_out, dq_rope_res, out_sem.at[1]),
    ]
    for store in stores:
        store.start()

    def sum_lines(c):
        def step(i):
            k = HALF - i

            @pl.when((k >= r_end(c)) & (k <= r_first(c)))
            def _():
                unit = r_unit(c, k)
                for j in (1, 2, 3):
                    rl(c, k, j).wait_recv()
                total = terms[unit, :, y] if c == 0 else terms[unit, x]
                total = total.astype(f32)
                for j in range(3):
                    total = total + line_in[k, j].astype(f32)
                if c == 0:
                    terms[unit, :, y] = total.astype(bf16)
                else:
                    terms[unit, x] = total.astype(bf16)
                for j in (2, 1, 3):
                    rp(c, k, j).start()

        each(0, HALF + 1, step)

    by_core(sum_lines)

    def sum_pieces(c):
        def step(i):
            k = HALF - i

            @pl.when((k >= r_end(c)) & (k <= r_first(c)))
            def _():
                unit = r_unit(c, k)
                for j in (1, 2, 3):
                    rp(c, k, j).wait_recv()
                total = terms[unit, x, y].astype(f32)
                for j in range(3):
                    total = total + piece_in[k, j].astype(f32)
                terms[unit, x, y] = total.astype(bf16)

                @pl.when(k >= 1)
                def _():
                    rz(c, k).start()

        each(0, HALF + 1, step)

    by_core(sum_pieces)

    def sum_ring(c):
        share[...] = jnp.zeros((PIECE, CAT), f32) if c == 0 else terms[z, x, y].astype(f32)

        def step(k):
            rz(c, k).wait_recv()
            share[...] += ring_in[k].astype(f32)

        each(1, r_first(c) + 1, step)

    by_core(sum_ring)

    holds = lax.rem(x, 2) == core
    half_of = lax.div(x, 2)

    def rh():
        return remote(share, share_in, rh_s.at[0], rh_r.at[0], sibling)

    def f1(j, back):
        ref = final.at[wrap(y - back, NP)]
        return remote(ref, ref, f1_s.at[j], f1_r.at[j], at_y(j))

    def f2(j, back):
        ref = result.at[lax.div(wrap(x - back, NP), 2)]
        return remote(final, ref, f2_s.at[j], f2_r.at[j], at_x(j))

    @pl.when(holds)
    def _():
        rh().wait_recv()
        final[y] = (share[...] + share_in[...]).astype(bf16)
        for j in (2, 1, 3):
            f1(j, 0).start()
        for j in (1, 2, 3):
            f1(j, j).wait_recv()
        for j in (2, 1, 3):
            f2(j, 0).start()
        result[half_of] = final[...]

    @pl.when(jnp.logical_not(holds))
    def _():
        rh().start()

    for j in (1, 2, 3):

        @pl.when(lax.rem(x + NP - j, 2) == core)
        def _():
            f2(j, j).wait_recv()

    gain_row = gain[...].astype(f32)
    kv_rows = kv_t[...].T
    grads = result[...].reshape(2 * SPAN, CAT).astype(f32)
    values = kv_rows[:, :LAT].astype(f32)
    inv = lax.rsqrt(jnp.mean(values * values, axis=-1, keepdims=True) + EPS_NORM)
    scaled = grads[:, :LAT] * gain_row
    inner = jnp.mean(values * scaled, axis=-1, keepdims=True)
    d_raw = inv * scaled - values * (inv * inv * inv * inner)
    d_cache_out[:LAT, :] = d_raw.T
    d_cache_out[LAT:, :] = grads[:, LAT:].T
    store = pltpu.make_async_copy(d_cache_out, d_cache_res, out_sem.at[2])
    store.start()

    for n in range(2):
        g_own(n).wait_send()

    def sends(c):
        def gather_step(d):
            gz(c, d, z).wait_send()
            for j in (1, 2, 3):
                gp(c, d, j, 0).wait_send()
                gl(c, d, j, 0).wait_send()
            gs(c, d).wait_send()

        each(1, g_last(c) + 1, gather_step)

        def reduce_twin(k):
            ra(1 - c, k).wait_send()

        each(r_end(1 - c), r_first(1 - c) + 1, reduce_twin)

        def reduce_step(k):
            for j in (1, 2, 3):
                rl(c, k, j).wait_send()
                rp(c, k, j).wait_send()

        each(r_end(c), r_first(c) + 1, reduce_step)
        each(1, r_first(c) + 1, lambda k: rz(c, k).wait_send())

    by_core(sends)

    @pl.when(holds)
    def _():
        for j in (1, 2, 3):
            f1(j, 0).wait_send()
            f2(j, 0).wait_send()

    @pl.when(jnp.logical_not(holds))
    def _():
        rh().wait_send()

    for done in stores:
        done.wait()
    store.wait()


def local(q_nope, q_rope, kv_cache, kv_gain, w_uk, w_uv, attn_out, d_out, span_table):
    toks = q_nope.shape[0]
    hbm = pl.BlockSpec(memory_space=pl.ANY)
    smem = pl.BlockSpec(memory_space=pltpu.SMEM)
    dma = pltpu.SemaphoreType.DMA
    inputs = (
        q_nope, q_rope, kv_cache.T, kv_gain.reshape(1, LAT), w_uk, w_uv, attn_out, d_out
    )
    out_shape = (
        jax.ShapeDtypeStruct((toks, HEADS * NOPE), bf16),
        jax.ShapeDtypeStruct((toks, HEADS * ROPE), bf16),
        jax.ShapeDtypeStruct((CAT, toks), f32),
    )
    scratch = [pltpu.VMEM(value.shape, value.dtype) for value in inputs]
    scratch += [pltpu.VMEM(value.shape, value.dtype) for value in out_shape]
    scratch += [
        pltpu.VMEM((NZ, NP, NP, PIECE, CAT), bf16),
        pltpu.VMEM((NZ, NP, NP, PIECE, CAT), bf16),
        pltpu.VMEM((HALF + 1, NP, NP, PIECE, CAT), bf16),
        pltpu.VMEM((HALF + 1, 3, NP, PIECE, CAT), bf16),
        pltpu.VMEM((HALF + 1, 3, PIECE, CAT), bf16),
        pltpu.VMEM((HALF + 1, PIECE, CAT), bf16),
        pltpu.VMEM((PIECE, CAT), f32),
        pltpu.VMEM((PIECE, CAT), f32),
        pltpu.VMEM((NP, PIECE, CAT), bf16),
        pltpu.VMEM((2, NP, PIECE, CAT), bf16),
        pltpu.VMEM((2, ROWS, CAT), bf16),
        pltpu.VMEM((2, ROWS, LAT), bf16),
        pltpu.VMEM((2, 1, ROWS), f32),
        pltpu.VMEM((FIRST + OTHER, CHUNK, ROWS), f32),
        pltpu.VMEM((FIRST + OTHER, CHUNK, ROWS), f32),
        pltpu.VMEM((OTHER + 1, 8, ROWS), f32),
        pltpu.VMEM((BLANK + 1, SPAN, CAT), f32),
        pltpu.VMEM((OTHER, ROWS, CAT), f32),
        pltpu.VMEM((ROWS, CAT), f32),
        pltpu.VMEM((2, 1, ROWS), f32),
        pltpu.VMEM((FIRST + OTHER, 8, ROWS), f32),
        pltpu.SMEM((2 * NZ,), jnp.int32),
        dma((len(inputs),)),
        dma((3,)),
        dma((2,)), dma((2,)),
        dma((HALF + 1,)), dma((HALF + 1,)),
        dma((HALF + 1, NP)), dma((HALF + 1, NP)),
        dma((HALF + 1, NP)), dma((HALF + 1, NP)),
        dma((HALF + 1,)), dma((HALF + 1,)),
        dma((HALF + 1,)), dma((HALF + 1,)),
        dma((HALF + 1, NP)), dma((HALF + 1, NP)),
        dma((HALF + 1, NP)), dma((HALF + 1, NP)),
        dma((HALF + 1,)), dma((HALF + 1,)),
        dma((1,)), dma((1,)),
        dma((NP,)), dma((NP,)),
        dma((NP,)), dma((NP,)),
    ]
    d_q_nope, d_q_rope, d_cache = pl.pallas_call(
        kernel,
        out_shape=out_shape,
        in_specs=[hbm] * len(inputs) + [smem],
        out_specs=(hbm, hbm, hbm),
        scratch_shapes=scratch,
        compiler_params=pltpu.CompilerParams(
            collective_id=0, has_side_effects=True, vmem_limit_bytes=60 * 1024 * 1024
        ),
    )(*inputs, span_table.T)
    return d_q_nope, d_q_rope, d_cache.T


def solution(mesh):
    in_specs = (
        P("ctx", "head"),
        P("ctx", "head"),
        P("ctx", None),
        P(),
        P("head", None, None),
        P("head", None, None),
        P("ctx", "head"),
        P("ctx", "head"),
        P(),
    )
    out_specs = (P("ctx", "head"), P("ctx", "head"), P("ctx", None))
    return jax.shard_map(local, mesh=mesh, in_specs=in_specs, out_specs=out_specs, check_vma=False)
```

```python
import functools

import jax
import jax.numpy as jnp
from jax import lax
from jax.experimental import pallas as pl
from jax.experimental.pallas import tpu as pltpu
from jax.sharding import PartitionSpec as P

MESH = pl.DeviceIdType.MESH
NEG_BIG = -1e30
EPS_NORM = 1e-06
LOG2_E = 1.4426950408889634

NZ = 16
HALF = NZ // 2
NP = 4
PIECE = 16
SPAN = 64
HEADS = 4
ROWS = SPAN * HEADS
LAT = 512
ROPE = 64
LAG_G = 4
LAG_R = 2
CAT = LAT + ROPE
NOPE = 128
CHUNK = 256
FIRST = 8
OTHER = 9
BLANK = 4 * OTHER

f32 = jnp.float32
bf16 = jnp.bfloat16


def dot(a, b, ca, cb):
    return lax.dot_general(a, b, (((ca,), (cb,)), ((), ())), preferred_element_type=f32)


def wrap(value, size):
    return lax.rem(value + 2 * size, size)


def kernel(
    q_nope_in, q_rope_in, kv_in, gain_in, w_uk_in, w_uv_in, attn_out_in, d_out_in, table,
    dq_nope_res, dq_rope_res, d_cache_res,
    q_nope, q_rope, kv_t, gain, w_uk, w_uv, attn_out, d_out,
    dq_nope_out, dq_rope_out, d_cache_out,
    keys, terms, sib_in, line_in, piece_in, ring_in, share, result,
    queries, d_latent, delta, scores, d_prob, tops, other_terms, dq_prefix, dq_first,
    stats, sums, inverse, in_sem, out_sem,
    g0_s, g0_r, gz_s, gz_r, gp_s, gp_r, gl_s, gl_r, gs_s, gs_r,
    ra_s, ra_r, rl_s, rl_r, rp_s, rp_r, rz_s, rz_r, f1_s, f1_r,
):
    scale = float(NOPE + ROPE) ** (-0.5)
    ctx = lax.axis_index("ctx")
    head = lax.axis_index("head")
    z, core = lax.div(ctx, 2), lax.rem(ctx, 2)
    x, y = lax.div(head, NP), lax.rem(head, NP)
    twin = 1 - core

    def at_x(j):
        return {"ctx": ctx, "head": wrap(x + j, NP) * NP + y}

    def at_y(j):
        return {"ctx": ctx, "head": x * NP + wrap(y + j, NP)}

    def at_z(zz):
        return {"ctx": zz * 2 + core, "head": head}

    sibling = {"ctx": z * 2 + twin, "head": head}

    def remote(src, dst, send, recv, device):
        return pltpu.make_async_remote_copy(
            src_ref=src, dst_ref=dst, send_sem=send, recv_sem=recv,
            device_id=device, device_id_type=MESH,
        )

    def by_core(step):
        for c in range(2):
            pl.when(core == c)(functools.partial(step, c))

    holds = lax.rem(x, 2) == core
    holder = lax.rem(x, 2)

    def at_plane(i, j):
        return {"ctx": ctx, "head": wrap(x + i, NP) * NP + wrap(y + j, NP)}

    barrier = pltpu.get_barrier_semaphore()

    def signal(device):
        pl.semaphore_signal(barrier, inc=1, device_id=device, device_id_type=MESH)

    def greet(c):
        for d in range(HALF if c == 0 else HALF - 1, 0, -1):
            signal({"ctx": wrap(z - d if c == 0 else z + d, NZ) * 2 + c, "head": head})

        @pl.when(holds)
        def _():
            for d in range(HALF - 1 if c == 0 else HALF, 0, -1):
                signal({"ctx": wrap(z + d if c == 0 else z - d, NZ) * 2 + 1 - c, "head": head})

    by_core(greet)
    for i in range(NP):
        for j in range(NP):
            if i and j:

                @pl.when(lax.rem(x + i, 2) == core)
                def _():
                    signal(at_plane(i, j))

            elif i or j:
                signal(at_plane(i, j))
    signal(sibling)

    loads = [
        pltpu.make_async_copy(src, dst, in_sem.at[n])
        for n, (src, dst) in enumerate(
            (
                (kv_in, kv_t), (gain_in, gain), (q_nope_in, q_nope), (w_uk_in, w_uk),
                (q_rope_in, q_rope), (d_out_in, d_out), (w_uv_in, w_uv), (attn_out_in, attn_out),
            )
        )
    ]
    for load in loads:
        load.start()

    loads[0].wait()
    loads[1].wait()
    kv = kv_t[...].T
    raw = kv[:, :LAT].astype(f32)
    inv_norm = lax.rsqrt(jnp.mean(raw * raw, axis=-1, keepdims=True) + EPS_NORM)
    latent = (raw * inv_norm * gain[...].reshape(1, LAT).astype(f32)).astype(bf16)
    own_rope = kv[:, LAT:]
    for half in range(2):
        rows = slice(half * SPAN, (half + 1) * SPAN)
        keys[z, 2 * half + core, :, :, :LAT] = latent[rows].reshape(NP, PIECE, LAT)
        keys[z, 2 * half + core, :, :, LAT:] = own_rope[rows].reshape(NP, PIECE, ROPE)

    for load in loads[2:]:
        load.wait()
    for h in range(HEADS):
        cols = slice(h * NOPE, (h + 1) * NOPE)
        rows = slice(h * SPAN, (h + 1) * SPAN)
        q_lat = dot(q_nope[:, cols], w_uk[h], 1, 0).astype(bf16)
        d_lat = dot(d_out[:, cols], w_uv[h], 1, 1).astype(bf16)
        for half in range(2):
            toks = slice(half * SPAN, (half + 1) * SPAN)
            queries[half, rows, :LAT] = q_lat[toks]
            queries[half, rows, LAT:] = q_rope[toks, h * ROPE : (h + 1) * ROPE]
            d_latent[half, rows, :] = d_lat[toks]
    for half in range(2):
        toks = slice(half * SPAN, (half + 1) * SPAN)
        prods = [
            d_out[toks, h * NOPE : (h + 1) * NOPE].astype(f32)
            * attn_out[toks, h * NOPE : (h + 1) * NOPE].astype(f32)
            for h in range(HEADS)
        ]
        prod = jnp.concatenate(prods, axis=0)
        delta[half] = jnp.sum(prod.T, axis=0, keepdims=True)

    tops[...] = jnp.full(tops.shape, NEG_BIG, f32)
    dq_first[...] = jnp.zeros(dq_first.shape, f32)
    other_terms[BLANK] = jnp.zeros((SPAN, CAT), f32)

    z_targets = HALF - core
    targets = 2 * (NP - 1) + 1 + z_targets
    pl.semaphore_wait(barrier, jnp.where(holds, targets + (NP - 1) ** 2, targets + z_targets))

    def g_last(c):
        return HALF if c == 0 else HALF - 1

    def g_unit(c, d):
        return wrap(z - d, NZ) if c == 0 else wrap(z + d, NZ)

    def g_own(n):
        ref = keys.at[z, 2 * n + core]
        return remote(ref, ref, g0_s.at[n], g0_r.at[n], sibling)

    def g_own_arrival(n):
        ref = keys.at[z, 2 * n + twin]
        return remote(ref, ref, g0_s.at[n], g0_r.at[n], sibling)

    def gz(c, d, unit):
        ref = keys.at[unit, x, y]
        device = at_z(wrap(z + d, NZ) if c == 0 else wrap(z - d, NZ))
        return remote(ref, ref, gz_s.at[d], gz_r.at[d], device)

    def gp(c, d, j, back):
        unit = g_unit(c, d)
        if c == 0:
            ref, device = keys.at[unit, wrap(x - back, NP), y], at_x(j)
        else:
            ref, device = keys.at[unit, x, wrap(y - back, NP)], at_y(j)
        return remote(ref, ref, gp_s.at[d, j], gp_r.at[d, j], device)

    def gl(c, d, j, back):
        unit = g_unit(c, d)
        if c == 0:
            ref, device = keys.at[unit, :, wrap(y - back, NP)], at_y(j)
        else:
            ref, device = keys.at[unit, wrap(x - back, NP)], at_x(j)
        return remote(ref, ref, gl_s.at[d, j], gl_r.at[d, j], device)

    def gs(c, d):
        ref = keys.at[g_unit(c, d)]
        return remote(ref, ref, gs_s.at[d], gs_r.at[d], sibling)

    for n in range(2):
        g_own(n).start()
    for n in range(2):
        g_own_arrival(n).wait_recv()

    def each(low, high, step):
        def body(d, carry):
            step(d)
            return carry

        lax.fori_loop(low, high, body, 0)

    def spread_z(c):
        each(1, g_last(c) + 1, lambda d: gz(c, d, z).start())

    by_core(spread_z)

    def invert(b, carry):
        found = jnp.int32(0)
        for d in range(2 * NZ):
            found = found + jnp.where(table[0, d] == b, d, 0)
        inverse[b] = jnp.minimum(found, 2 * NZ - 1)
        return carry

    lax.fori_loop(0, 2 * NZ, invert, 0)
    mine = table[0, ctx]
    low_chunks = lax.div(mine + 4, 4)

    def spread(c):
        def step(d):
            @pl.when(d <= g_last(c))
            def _():
                gz(c, d, g_unit(c, d)).wait_recv()
                for j in (2, 1, 3):
                    gp(c, d, j, 0).start()

            e = d - LAG_G

            @pl.when(e >= 1)
            def _():
                for j in (1, 2, 3):
                    gp(c, e, j, j).wait_recv()
                for j in (2, 1, 3):
                    gl(c, e, j, 0).start()

        each(1, g_last(c) + LAG_G + 1, step)

    by_core(spread)

    def first_keys(t):
        low = keys[wrap(z - t, NZ), 0:2].reshape(CHUNK // 2, CAT)
        high = keys[wrap(z + lax.rem(t, HALF), NZ), 0:2].reshape(CHUNK // 2, CAT)
        return jnp.concatenate([low, high], axis=0)

    def fold_rows(value, op):
        part = value[0:8]
        for r in range(8, value.shape[0], 8):
            part = op(part, value[r : r + 8])
        return part

    def arrivals(d):
        def own(c):
            @pl.when(d <= g_last(c))
            def _():
                for j in (1, 2, 3):
                    gl(c, d, j, j).wait_recv()
                gs(c, d).start()

            @pl.when((d >= 2) & (d - 1 <= g_last(1 - c)))
            def _():
                gs(1 - c, d - 1).wait_recv()

        by_core(own)

        @pl.when(d >= 2)
        def _():
            t = d - 1
            chunk = first_keys(t)
            part = dot(chunk, queries[1], 1, 1)
            scores[t - 1] = part
            tops[OTHER] = jnp.maximum(tops[OTHER], fold_rows(part, jnp.maximum))
            d_prob[t - 1] = dot(chunk[:, :LAT], d_latent[1], 1, 1)

    each(1, HALF + 2, arrivals)

    def kind_of(j):
        return jnp.where(j >= low_chunks, 1, 0)

    def other_keys(j):
        kind = kind_of(j)
        blocks = []
        for i in range(4):
            low_id = inverse[jnp.minimum(4 * j + i, 2 * NZ - 1)]
            high_id = inverse[jnp.clip(2 * NZ - 1 - (4 * (j - low_chunks) + i), 0, 2 * NZ - 1)]
            owner = jnp.where(kind == 1, high_id, low_id)
            block = keys[lax.div(owner, 2), 2 * kind + lax.rem(owner, 2)]
            blocks.append(block.reshape(SPAN, CAT))
        return jnp.concatenate(blocks, axis=0)

    key_in = lax.broadcasted_iota(jnp.int32, (CHUNK, ROWS), 0)
    tok_in = lax.rem(lax.broadcasted_iota(jnp.int32, (CHUNK, ROWS), 1), SPAN)

    def other_scores(j, carry):
        kind = kind_of(j)
        chunk = other_keys(j)
        low_gap = (4 * j - mine) * SPAN
        high_gap = (4 * (j - low_chunks) - (2 * NZ - 1 - mine)) * SPAN
        gap = jnp.where(kind == 1, high_gap, low_gap)
        part = dot(chunk, queries[kind], 1, 1)
        part = jnp.where(key_in + gap <= tok_in, part, NEG_BIG)
        scores[FIRST + j] = part
        tops[j] = fold_rows(part, jnp.maximum)
        d_prob[FIRST + j] = dot(chunk[:, :LAT], d_latent[kind], 1, 1)
        return carry

    lax.fori_loop(0, OTHER, other_scores, 0)

    top_low = jnp.full((8, ROWS), NEG_BIG, f32)
    top_high = tops[OTHER]
    for j in range(OTHER):
        high = j >= low_chunks
        top_low = jnp.maximum(top_low, jnp.where(high, NEG_BIG, tops[j]))
        top_high = jnp.maximum(top_high, jnp.where(high, tops[j], NEG_BIG))
    rate = scale * LOG2_E
    stats[0] = jnp.max(top_low, axis=0, keepdims=True) * rate
    stats[1] = jnp.max(top_high, axis=0, keepdims=True) * rate

    def exponents(n, carry):
        kind = jnp.where(n < FIRST, 1, kind_of(n - FIRST))
        part = jnp.exp2(scores[n] * rate - stats[kind])
        scores[n] = part
        sums[n] = fold_rows(part, jnp.add)
        return carry

    lax.fori_loop(0, FIRST + OTHER, exponents, 0)

    sum_low = jnp.zeros((8, ROWS), f32)
    sum_high = jnp.zeros((8, ROWS), f32)
    for n in range(FIRST):
        sum_high = sum_high + sums[n]
    for j in range(OTHER):
        high = j >= low_chunks
        sum_low = sum_low + jnp.where(high, 0.0, sums[FIRST + j])
        sum_high = sum_high + jnp.where(high, sums[FIRST + j], 0.0)
    stats[0] = 1.0 / jnp.sum(sum_low, axis=0, keepdims=True)
    stats[1] = 1.0 / jnp.sum(sum_high, axis=0, keepdims=True)

    def chunk_grads(n, kind, chunk):
        expo = scores[n]
        inv_sum = stats[kind]
        prob = (expo * inv_sum).astype(bf16)
        d_score = ((d_prob[n] - delta[kind]) * (expo * (inv_sum * scale))).astype(bf16)
        dq = dot(d_score, chunk, 0, 0)
        dk = dot(d_score, queries[kind], 1, 0)
        dk_lat = dk[:, :LAT] + dot(prob, d_latent[kind], 1, 0)
        return dq, dk_lat, dk[:, LAT:]

    def other_grads(j, carry):
        dq, dk_lat, dk_rope = chunk_grads(FIRST + j, kind_of(j), other_keys(j))
        for i in range(4):
            rows = slice(i * SPAN, (i + 1) * SPAN)
            other_terms[4 * j + i, :, :LAT] = dk_lat[rows]
            other_terms[4 * j + i, :, LAT:] = dk_rope[rows]

        fresh = (j == 0) | (j == low_chunks)
        before = dq_prefix[jnp.maximum(j - 1, 0)]
        dq_prefix[j] = dq + jnp.where(fresh, 0.0, before)
        return carry

    dq_prefix[0] = jnp.zeros((ROWS, CAT), f32)
    lax.fori_loop(0, OTHER, other_grads, 0)

    def r_first(c):
        return HALF if c == 0 else HALF - 1

    def r_end(c):
        return 1 if c == 0 else 0

    def r_unit(c, k):
        return wrap(z + k, NZ) if c == 0 else wrap(z - k, NZ)

    def ra(c, k):
        return remote(terms.at[r_unit(c, k)], sib_in.at[k], ra_s.at[k], ra_r.at[k], sibling)

    def rl(c, k, j):
        unit = r_unit(c, k)
        if c == 0:
            ref, device = terms.at[unit, :, wrap(y + j, NP)], at_y(j)
        else:
            ref, device = terms.at[unit, wrap(x + j, NP)], at_x(j)
        return remote(ref, line_in.at[k, j - 1], rl_s.at[k, j], rl_r.at[k, j], device)

    def rp(c, k, j):
        unit = r_unit(c, k)
        if c == 0:
            ref, device = terms.at[unit, wrap(x + j, NP), y], at_x(j)
        else:
            ref, device = terms.at[unit, x, wrap(y + j, NP)], at_y(j)
        return remote(ref, piece_in.at[k, j - 1], rp_s.at[k, j], rp_r.at[k, j], device)

    def rz(c, k):
        unit = r_unit(c, k)
        device = {"ctx": unit * 2 + holder, "head": head}
        return remote(terms.at[unit, x, y], ring_in.at[c, k], rz_s.at[k], rz_r.at[c, k], device)

    def first_grads(k):
        n = k - 1
        dq, dk_lat, dk_rope = chunk_grads(n, 1, first_keys(k))
        dq_first[...] += dq
        units = (wrap(z - k, NZ), wrap(z + lax.rem(k, HALF), NZ))
        for s in range(2):
            unit = units[s]
            for cc in range(2):
                block = table[0, unit * 2 + cc]
                low_slot = jnp.where(block < 4 * low_chunks, block, BLANK)
                high_slot = jnp.minimum(4 * low_chunks + (2 * NZ - 1 - block), BLANK)
                low_term = other_terms[low_slot]
                rows = slice((2 * s + cc) * SPAN, (2 * s + cc + 1) * SPAN)
                terms[unit, cc, :, :, :LAT] = (
                    (dk_lat[rows] + low_term[:, :LAT]).astype(bf16).reshape(NP, PIECE, LAT)
                )
                terms[unit, cc, :, :, LAT:] = (
                    (dk_rope[rows] + low_term[:, LAT:]).astype(bf16).reshape(NP, PIECE, ROPE)
                )
                terms[unit, 2 + cc] = other_terms[high_slot].astype(bf16).reshape(NP, PIECE, CAT)

    def reduce_step(i):
        @pl.when(i < HALF)
        def _():
            first_grads(HALF - i)

        k = HALF - i

        def own(c):
            @pl.when((k >= r_end(1 - c)) & (k <= r_first(1 - c)))
            def _():
                ra(1 - c, k).start()

            ka = k + 1

            @pl.when((ka >= r_end(c)) & (ka <= r_first(c)))
            def _():
                unit = r_unit(c, ka)
                ra(c, ka).wait_recv()
                both = terms[unit].astype(f32) + sib_in[ka].astype(f32)
                terms[unit] = both.astype(bf16)
                for j in (2, 1, 3):
                    rl(c, ka, j).start()

        by_core(own)

    each(0, HALF + 2, reduce_step)

    low = dq_prefix[low_chunks - 1]
    high = dq_prefix[OTHER - 1] + dq_first[...]
    for half, part in ((0, low), (1, high)):
        toks = slice(half * SPAN, (half + 1) * SPAN)
        dq_lat = part[:, :LAT].astype(bf16)
        dq_rope = part[:, LAT:]
        for h in range(HEADS):
            rows = slice(h * SPAN, (h + 1) * SPAN)
            dq_nope_out[toks, h * NOPE : (h + 1) * NOPE] = dot(
                dq_lat[rows], w_uk[h], 1, 1
            ).astype(bf16)
        for h in range(0, HEADS, 2):
            pair = jnp.concatenate(
                [dq_rope[h * SPAN : (h + 1) * SPAN], dq_rope[(h + 1) * SPAN : (h + 2) * SPAN]],
                axis=1,
            )
            dq_rope_out[toks, h * ROPE : (h + 2) * ROPE] = pair.astype(bf16)
    stores = [
        pltpu.make_async_copy(dq_nope_out, dq_nope_res, out_sem.at[0]),
        pltpu.make_async_copy(dq_rope_out, dq_rope_res, out_sem.at[1]),
    ]
    for store in stores:
        store.start()

    def sum_line(c, k):
        unit = r_unit(c, k)
        for j in (1, 2, 3):
            rl(c, k, j).wait_recv()
        total = terms[unit, :, y] if c == 0 else terms[unit, x]
        total = total.astype(f32)
        for j in range(3):
            total = total + line_in[k, j].astype(f32)
        if c == 0:
            terms[unit, :, y] = total.astype(bf16)
        else:
            terms[unit, x] = total.astype(bf16)
        for j in (2, 1, 3):
            rp(c, k, j).start()

    def sum_piece(c, k):
        unit = r_unit(c, k)
        for j in (1, 2, 3):
            rp(c, k, j).wait_recv()
        total = terms[unit, x, y].astype(f32)
        for j in range(3):
            total = total + piece_in[k, j].astype(f32)
        terms[unit, x, y] = total.astype(bf16)

        if c == 0:
            rz(c, k).start()
        else:
            kept = (k == 0) & holds

            @pl.when(kept)
            def _():
                ring_in[c, 0] = terms[unit, x, y]

            @pl.when(jnp.logical_not(kept))
            def _():
                rz(c, k).start()

    def sum_over_plane(c):
        def step(i):
            k = HALF - i

            @pl.when((k >= r_end(c)) & (k <= r_first(c)))
            def _():
                sum_line(c, k)

            late = k + LAG_R

            @pl.when((late >= r_end(c)) & (late <= r_first(c)))
            def _():
                sum_piece(c, late)

        each(0, HALF + 1 + LAG_R, step)

    by_core(sum_over_plane)

    def f1(i, j, back):
        if back:
            xs, ys = wrap(x - i, NP), wrap(y - j, NP)
        else:
            xs, ys = x, y
        ref = result.at[lax.div(xs, 2), ys]
        return remote(ref, ref, f1_s.at[i, j], f1_r.at[i, j], at_plane(i, j))

    far_first = sorted(
        ((i, j) for i in range(NP) for j in range(NP) if i or j),
        key=lambda ij: -(min(ij[0], NP - ij[0]) + min(ij[1], NP - ij[1])),
    )

    @pl.when(holds)
    def _():
        share[...] = jnp.zeros((PIECE, CAT), f32)
        for c in range(2):

            def step(i, c=c):
                k = HALF - i

                @pl.when((k >= r_end(c)) & (k <= r_first(c)))
                def _():
                    @pl.when(jnp.logical_not((k == 0) & (core == 1)))
                    def _():
                        rz(c, k).wait_recv()

                    share[...] += ring_in[c, k].astype(f32)

            each(0, HALF + 1, step)
        result[lax.div(x, 2), y] = share[...].astype(bf16)
        for i, j in far_first:
            f1(i, j, False).start()

    for i, j in reversed(far_first):

        @pl.when(lax.rem(x + NP - i, 2) == core)
        def _():
            f1(i, j, True).wait_recv()

    gain_row = gain[...].reshape(1, LAT).astype(f32)
    kv_rows = kv_t[...].T
    grads = result[...].reshape(2 * SPAN, CAT).astype(f32)
    values = kv_rows[:, :LAT].astype(f32)
    inv = lax.rsqrt(jnp.mean(values * values, axis=-1, keepdims=True) + EPS_NORM)
    scaled = grads[:, :LAT] * gain_row
    inner = jnp.mean(values * scaled, axis=-1, keepdims=True)
    d_raw = inv * scaled - values * (inv * inv * inv * inner)
    d_cache_out[:LAT, :] = d_raw.T
    d_cache_out[LAT:, :] = grads[:, LAT:].T
    store = pltpu.make_async_copy(d_cache_out, d_cache_res, out_sem.at[2])
    store.start()

    for n in range(2):
        g_own(n).wait_send()

    def sends(c):
        def gather_step(d):
            gz(c, d, z).wait_send()
            for j in (1, 2, 3):
                gp(c, d, j, 0).wait_send()
                gl(c, d, j, 0).wait_send()
            gs(c, d).wait_send()

        each(1, g_last(c) + 1, gather_step)

        def reduce_twin(k):
            ra(1 - c, k).wait_send()

        each(r_end(1 - c), r_first(1 - c) + 1, reduce_twin)

        def reduce_step(k):
            for j in (1, 2, 3):
                rl(c, k, j).wait_send()
                rp(c, k, j).wait_send()

        each(r_end(c), r_first(c) + 1, reduce_step)
        each(1, r_first(c) + 1, lambda k: rz(c, k).wait_send())
        if c == 1:

            @pl.when(jnp.logical_not(holds))
            def _():
                rz(c, 0).wait_send()

    by_core(sends)

    @pl.when(holds)
    def _():
        for i, j in far_first:
            f1(i, j, False).wait_send()

    for done in stores:
        done.wait()
    store.wait()


def hand_over(*refs):
    for src, dst in zip(refs[:3], refs[3:]):
        dst[...] = src[...]


def local(q_nope, q_rope, kv_cache, kv_gain, w_uk, w_uv, attn_out, d_out, span_table):
    toks = q_nope.shape[0]
    hbm = pl.BlockSpec(memory_space=pl.ANY)
    smem = pl.BlockSpec(memory_space=pltpu.SMEM)
    vmem = pl.BlockSpec(memory_space=pltpu.VMEM)
    dma = pltpu.SemaphoreType.DMA
    inputs = (
        q_nope, q_rope, kv_cache.T, kv_gain, w_uk, w_uv, attn_out, d_out
    )
    out_shape = (
        jax.ShapeDtypeStruct((toks, HEADS * NOPE), bf16),
        jax.ShapeDtypeStruct((toks, HEADS * ROPE), bf16),
        jax.ShapeDtypeStruct((CAT, toks), f32),
    )
    scratch = [pltpu.VMEM(value.shape, value.dtype) for value in inputs]
    scratch += [pltpu.VMEM(value.shape, value.dtype) for value in out_shape]
    scratch += [
        pltpu.VMEM((NZ, NP, NP, PIECE, CAT), bf16),
        pltpu.VMEM((NZ, NP, NP, PIECE, CAT), bf16),
        pltpu.VMEM((HALF + 1, NP, NP, PIECE, CAT), bf16),
        pltpu.VMEM((HALF + 1, 3, NP, PIECE, CAT), bf16),
        pltpu.VMEM((HALF + 1, 3, PIECE, CAT), bf16),
        pltpu.VMEM((2, HALF + 1, PIECE, CAT), bf16),
        pltpu.VMEM((PIECE, CAT), f32),
        pltpu.VMEM((2, NP, PIECE, CAT), bf16),
        pltpu.VMEM((2, ROWS, CAT), bf16),
        pltpu.VMEM((2, ROWS, LAT), bf16),
        pltpu.VMEM((2, 1, ROWS), f32),
        pltpu.VMEM((FIRST + OTHER, CHUNK, ROWS), f32),
        pltpu.VMEM((FIRST + OTHER, CHUNK, ROWS), f32),
        pltpu.VMEM((OTHER + 1, 8, ROWS), f32),
        pltpu.VMEM((BLANK + 1, SPAN, CAT), f32),
        pltpu.VMEM((OTHER, ROWS, CAT), f32),
        pltpu.VMEM((ROWS, CAT), f32),
        pltpu.VMEM((2, 1, ROWS), f32),
        pltpu.VMEM((FIRST + OTHER, 8, ROWS), f32),
        pltpu.SMEM((2 * NZ,), jnp.int32),
        dma((len(inputs),)),
        dma((3,)),
        dma((2,)), dma((2,)),
        dma((HALF + 1,)), dma((HALF + 1,)),
        dma((HALF + 1, NP)), dma((HALF + 1, NP)),
        dma((HALF + 1, NP)), dma((HALF + 1, NP)),
        dma((HALF + 1,)), dma((HALF + 1,)),
        dma((HALF + 1,)), dma((HALF + 1,)),
        dma((HALF + 1, NP)), dma((HALF + 1, NP)),
        dma((HALF + 1, NP)), dma((HALF + 1, NP)),
        dma((HALF + 1,)), dma((2, HALF + 1)),
        dma((NP, NP)), dma((NP, NP)),
    ]
    results = pl.pallas_call(
        kernel,
        out_shape=out_shape,
        in_specs=[hbm] * len(inputs) + [smem],
        out_specs=(hbm, hbm, hbm),
        scratch_shapes=scratch,
        compiler_params=pltpu.CompilerParams(
            collective_id=0, has_side_effects=True, vmem_limit_bytes=60 * 1024 * 1024
        ),
    )(*inputs, span_table.T)
    d_q_nope, d_q_rope, d_cache = pl.pallas_call(
        hand_over,
        out_shape=out_shape,
        in_specs=[vmem] * 3,
        out_specs=(vmem, vmem, vmem),
        compiler_params=pltpu.CompilerParams(vmem_limit_bytes=60 * 1024 * 1024),
    )(*results)
    return d_q_nope, d_q_rope, d_cache.T


def solution(mesh):
    in_specs = (
        P("ctx", "head"),
        P("ctx", "head"),
        P("ctx", None),
        P(),
        P("head", None, None),
        P("head", None, None),
        P("ctx", "head"),
        P("ctx", "head"),
        P(),
    )
    out_specs = (P("ctx", "head"), P("ctx", "head"), P("ctx", None))
    return jax.shard_map(local, mesh=mesh, in_specs=in_specs, out_specs=out_specs, check_vma=False)
```

```python
import functools

import jax
import jax.numpy as jnp
from jax import lax
from jax.experimental import pallas as pl
from jax.experimental.pallas import tpu as pltpu
from jax.sharding import PartitionSpec as P

MESH = pl.DeviceIdType.MESH
NEG_BIG = -1e30
EPS_NORM = 1e-06
LOG2_E = 1.4426950408889634

NZ = 16
HALF = NZ // 2
NP = 4
PIECE = 16
SPAN = 64
HEADS = 4
ROWS = SPAN * HEADS
LAT = 512
ROPE = 64
LAG_G = 4
NEAR = 2
LAG_R = 2
CAT = LAT + ROPE
NOPE = 128
CHUNK = 256
FIRST = 8
OTHER = 9
OWN_LOW = 2 * NZ
HIDDEN = OWN_LOW + 1
BLANK = 4 * OTHER

f32 = jnp.float32
bf16 = jnp.bfloat16


def dot(a, b, ca, cb):
    return lax.dot_general(a, b, (((ca,), (cb,)), ((), ())), preferred_element_type=f32)


def wrap(value, size):
    return lax.rem(value + 2 * size, size)


def kernel(
    q_nope_in, q_rope_in, kv_in, gain_in, w_uk_in, w_uv_in, attn_out_in, d_out_in, table,
    dq_nope_res, dq_rope_res, d_cache_res,
    q_nope, q_rope, kv_t, gain, w_uk, w_uv, attn_out, d_out,
    dq_nope_out, dq_rope_out, d_cache_out,
    keys, terms, sib_in, line_in, piece_in, ring_in, whole_in, share, result,
    queries, d_latent, delta, scores, d_prob, other_scores, other_prob, tops, other_terms, dq_prefix, dq_first,
    stats, sums, inverse, in_sem, out_sem,
    g0_s, g0_r, gz_s, gz_r, gp_s, gp_r, gl_s, gl_r, gs_s, gs_r,
    ra_s, ra_r, rl_s, rl_r, rp_s, rp_r, rz_s, rz_r, rw_s, rw_r, f1_s, f1_r,
):
    scale = float(NOPE + ROPE) ** (-0.5)
    ctx = lax.axis_index("ctx")
    head = lax.axis_index("head")
    z, core = lax.div(ctx, 2), lax.rem(ctx, 2)
    x, y = lax.div(head, NP), lax.rem(head, NP)
    twin = 1 - core

    def at_x(j):
        return {"ctx": ctx, "head": wrap(x + j, NP) * NP + y}

    def at_y(j):
        return {"ctx": ctx, "head": x * NP + wrap(y + j, NP)}

    def at_z(zz):
        return {"ctx": zz * 2 + core, "head": head}

    sibling = {"ctx": z * 2 + twin, "head": head}

    def remote(src, dst, send, recv, device):
        return pltpu.make_async_remote_copy(
            src_ref=src, dst_ref=dst, send_sem=send, recv_sem=recv,
            device_id=device, device_id_type=MESH,
        )

    def by_core(step):
        for c in range(2):
            pl.when(core == c)(functools.partial(step, c))

    holds = lax.rem(x, 2) == core
    holder = lax.rem(x, 2)

    def at_plane(i, j):
        return {"ctx": ctx, "head": wrap(x + i, NP) * NP + wrap(y + j, NP)}

    barrier = pltpu.get_barrier_semaphore()

    def signal(device):
        pl.semaphore_signal(barrier, inc=1, device_id=device, device_id_type=MESH)

    def greet(c):
        for d in range(HALF if c == 0 else HALF - 1, 0, -1):
            signal({"ctx": wrap(z - d if c == 0 else z + d, NZ) * 2 + c, "head": head})
        if c == 1:
            signal({"ctx": wrap(z - 1, NZ) * 2, "head": head})

        @pl.when(holds)
        def _():
            for d in range(HALF - 1 if c == 0 else HALF, 1, -1):
                signal({"ctx": wrap(z + d if c == 0 else z - d, NZ) * 2 + 1 - c, "head": head})

    by_core(greet)
    for i in range(NP):
        for j in range(NP):
            if i and j:

                @pl.when(lax.rem(x + i, 2) == core)
                def _():
                    signal(at_plane(i, j))

            elif i or j:
                signal(at_plane(i, j))
    signal(sibling)

    loads = [
        pltpu.make_async_copy(src, dst, in_sem.at[n])
        for n, (src, dst) in enumerate(
            (
                (kv_in, kv_t), (gain_in, gain), (q_nope_in, q_nope), (w_uk_in, w_uk),
                (q_rope_in, q_rope), (d_out_in, d_out), (w_uv_in, w_uv), (attn_out_in, attn_out),
            )
        )
    ]
    for load in loads:
        load.start()

    loads[0].wait()
    loads[1].wait()
    kv = kv_t[...].T
    raw = kv[:, :LAT].astype(f32)
    inv_norm = lax.rsqrt(jnp.mean(raw * raw, axis=-1, keepdims=True) + EPS_NORM)
    latent = (raw * inv_norm * gain[...].reshape(1, LAT).astype(f32)).astype(bf16)
    own_rope = kv[:, LAT:]
    for half in range(2):
        rows = slice(half * SPAN, (half + 1) * SPAN)
        keys[z, 2 * half + core, :, :, :LAT] = latent[rows].reshape(NP, PIECE, LAT)
        keys[z, 2 * half + core, :, :, LAT:] = own_rope[rows].reshape(NP, PIECE, ROPE)

    for load in loads[2:]:
        load.wait()
    for h in range(HEADS):
        cols = slice(h * NOPE, (h + 1) * NOPE)
        rows = slice(h * SPAN, (h + 1) * SPAN)
        q_lat = dot(q_nope[:, cols], w_uk[h], 1, 0).astype(bf16)
        d_lat = dot(d_out[:, cols], w_uv[h], 1, 1).astype(bf16)
        for half in range(2):
            toks = slice(half * SPAN, (half + 1) * SPAN)
            queries[half, rows, :LAT] = q_lat[toks]
            queries[half, rows, LAT:] = q_rope[toks, h * ROPE : (h + 1) * ROPE]
            d_latent[half, rows, :] = d_lat[toks]
    for half in range(2):
        toks = slice(half * SPAN, (half + 1) * SPAN)
        prods = [
            d_out[toks, h * NOPE : (h + 1) * NOPE].astype(f32)
            * attn_out[toks, h * NOPE : (h + 1) * NOPE].astype(f32)
            for h in range(HEADS)
        ]
        prod = jnp.concatenate(prods, axis=0)
        delta[half] = jnp.sum(prod.T, axis=0, keepdims=True)

    tops[...] = jnp.full(tops.shape, NEG_BIG, f32)
    dq_first[...] = jnp.zeros(dq_first.shape, f32)
    other_terms[BLANK] = jnp.zeros((SPAN, CAT), f32)
    other_scores[HIDDEN] = jnp.full((SPAN, ROWS), NEG_BIG, f32)
    other_prob[HIDDEN] = jnp.zeros((SPAN, ROWS), f32)

    targets = 2 * (NP - 1) + 1
    held = targets + (NP - 1) ** 2 + (HALF + 1) - 2 * core
    given = targets + 2 * HALF - 3 * core
    pl.semaphore_wait(barrier, jnp.where(holds, held, given))

    def g_last(c):
        return HALF if c == 0 else HALF - 1

    def g_unit(c, d):
        return wrap(z - d, NZ) if c == 0 else wrap(z + d, NZ)

    def g_own(n):
        ref = keys.at[z, 2 * n + core]
        return remote(ref, ref, g0_s.at[n], g0_r.at[n], sibling)

    def g_own_arrival(n):
        ref = keys.at[z, 2 * n + twin]
        return remote(ref, ref, g0_s.at[n], g0_r.at[n], sibling)

    def gz(c, d, unit, form="piece"):
        if form == "unit":
            ref = keys.at[unit]
        elif form == "line":
            ref = keys.at[unit, :, y] if c == 0 else keys.at[unit, x]
        else:
            ref = keys.at[unit, x, y]
        device = at_z(wrap(z + d, NZ) if c == 0 else wrap(z - d, NZ))
        return remote(ref, ref, gz_s.at[d], gz_r.at[d], device)

    def gp(c, d, j, back):
        unit = g_unit(c, d)
        if c == 0:
            ref, device = keys.at[unit, wrap(x - back, NP), y], at_x(j)
        else:
            ref, device = keys.at[unit, x, wrap(y - back, NP)], at_y(j)
        return remote(ref, ref, gp_s.at[d, j], gp_r.at[d, j], device)

    def gl(c, d, j, back):
        unit = g_unit(c, d)
        if c == 0:
            ref, device = keys.at[unit, :, wrap(y - back, NP)], at_y(j)
        else:
            ref, device = keys.at[unit, wrap(x - back, NP)], at_x(j)
        return remote(ref, ref, gl_s.at[d, j], gl_r.at[d, j], device)

    def gs(c, d):
        ref = keys.at[g_unit(c, d)]
        return remote(ref, ref, gs_s.at[d], gs_r.at[d], sibling)

    for n in range(2):
        g_own(n).start()
    for n in range(2):
        g_own_arrival(n).wait_recv()

    def each(low, high, step):
        def body(d, carry):
            step(d)
            return carry

        lax.fori_loop(low, high, body, 0)

    def spread_z(c):
        each(NEAR + 1, g_last(c) + 1, lambda d: gz(c, g_last(c) + NEAR + 1 - d, z).start())
        each(2, NEAR + 1, lambda d: gz(c, d, z, "line").start())
        gz(c, 1, z, "unit").start()

    by_core(spread_z)

    def invert(b, carry):
        found = jnp.int32(0)
        for d in range(2 * NZ):
            found = found + jnp.where(table[0, d] == b, d, 0)
        inverse[b] = jnp.minimum(found, 2 * NZ - 1)
        return carry

    lax.fori_loop(0, 2 * NZ, invert, 0)
    mine = table[0, ctx]
    low_chunks = lax.div(mine + 4, 4)

    def spread(c):
        def near_step(d):
            gz(c, d, g_unit(c, d), "line").wait_recv()
            for j in (2, 1, 3):
                gl(c, d, j, 0).start()

        each(2, NEAR + 1, near_step)

        def step(d):
            @pl.when(d <= g_last(c))
            def _():
                gz(c, d, g_unit(c, d)).wait_recv()
                for j in (2, 1, 3):
                    gp(c, d, j, 0).start()

            e = d - LAG_G

            @pl.when(e >= NEAR + 1)
            def _():
                for j in (1, 2, 3):
                    gp(c, e, j, j).wait_recv()
                for j in (2, 1, 3):
                    gl(c, e, j, 0).start()

        each(NEAR + 1, g_last(c) + LAG_G + 1, step)

    by_core(spread)

    def first_keys(t):
        low = keys[wrap(z - t, NZ), 0:2].reshape(CHUNK // 2, CAT)
        high = keys[wrap(z + lax.rem(t, HALF), NZ), 0:2].reshape(CHUNK // 2, CAT)
        return jnp.concatenate([low, high], axis=0)

    def fold_rows(value, op):
        part = value[0:8]
        for r in range(8, value.shape[0], 8):
            part = op(part, value[r : r + 8])
        return part

    key_in = lax.broadcasted_iota(jnp.int32, (SPAN, ROWS), 0)
    tok_in = lax.rem(lax.broadcasted_iota(jnp.int32, (SPAN, ROWS), 1), SPAN)

    own_low = keys[z, core].reshape(SPAN, CAT)
    own_part = jnp.where(key_in <= tok_in, dot(own_low, queries[0], 1, 1), NEG_BIG)
    other_scores[OWN_LOW] = own_part
    other_prob[OWN_LOW] = dot(own_low[:, :LAT], d_latent[0], 1, 1)
    tops[0] = fold_rows(own_part, jnp.maximum)

    def arrivals(d):
        def own(c):
            @pl.when(d == 1)
            def _():
                gz(c, 1, g_unit(c, 1), "unit").wait_recv()

            @pl.when((d >= 2) & (d <= g_last(c)))
            def _():
                for j in (1, 2, 3):
                    gl(c, d, j, j).wait_recv()

            @pl.when(d <= g_last(c))
            def _():
                gs(c, d).start()

            @pl.when((d >= 2) & (d - 1 <= g_last(1 - c)))
            def _():
                gs(1 - c, d - 1).wait_recv()

        by_core(own)

        @pl.when(d >= 2)
        def _():
            t = d - 1
            chunk = first_keys(t)
            part = dot(chunk, queries[1], 1, 1)
            scores[t - 1] = part
            tops[1] = jnp.maximum(tops[1], fold_rows(part, jnp.maximum))
            d_prob[t - 1] = dot(chunk[:, :LAT], d_latent[1], 1, 1)

            slots, kinds, blocks = [], [], []
            for unit in (wrap(z - t, NZ), wrap(z + lax.rem(t, HALF), NZ)):
                for cc in range(2):
                    slot = unit * 2 + cc
                    kind = jnp.where(table[0, slot] >= mine, 1, 0)
                    slots.append(slot)
                    kinds.append(kind)
                    block = jnp.where(kind == 1, keys[unit, 2 + cc], keys[unit, cc])
                    blocks.append(block.reshape(SPAN, CAT))
            chunk = jnp.concatenate(blocks, axis=0)
            part = [dot(chunk, queries[kind], 1, 1) for kind in range(2)]
            d_part = [dot(chunk[:, :LAT], d_latent[kind], 1, 1) for kind in range(2)]
            for n in range(4):
                rows = slice(n * SPAN, (n + 1) * SPAN)
                high = kinds[n] == 1
                block = jnp.where(high, part[1][rows], part[0][rows])
                gap = jnp.where(slots[n] == ctx, 0, -SPAN)
                block = jnp.where(key_in + gap <= tok_in, block, NEG_BIG)
                other_scores[slots[n]] = block
                other_prob[slots[n]] = jnp.where(high, d_part[1][rows], d_part[0][rows])
                top = fold_rows(block, jnp.maximum)
                tops[0] = jnp.maximum(tops[0], jnp.where(high, NEG_BIG, top))
                tops[1] = jnp.maximum(tops[1], jnp.where(high, top, NEG_BIG))

    each(1, HALF + 2, arrivals)

    def kind_of(j):
        return jnp.where(j >= low_chunks, 1, 0)

    def other_keys(j):
        kind = kind_of(j)
        blocks = []
        for i in range(4):
            low_id = inverse[jnp.minimum(4 * j + i, 2 * NZ - 1)]
            high_id = inverse[jnp.clip(2 * NZ - 1 - (4 * (j - low_chunks) + i), 0, 2 * NZ - 1)]
            owner = jnp.where(kind == 1, high_id, low_id)
            block = keys[lax.div(owner, 2), 2 * kind + lax.rem(owner, 2)]
            blocks.append(block.reshape(SPAN, CAT))
        return jnp.concatenate(blocks, axis=0)

    def other_slots(j):
        slots = []
        for i in range(4):
            low = 4 * j + i
            low_slot = inverse[jnp.minimum(low, 2 * NZ - 1)]
            low_slot = jnp.where(low < mine, low_slot, jnp.where(low == mine, OWN_LOW, HIDDEN))
            high = 2 * NZ - 1 - (4 * (j - low_chunks) + i)
            high_slot = inverse[jnp.clip(high, 0, 2 * NZ - 1)]
            high_slot = jnp.where(high >= mine, high_slot, HIDDEN)
            slots.append(jnp.where(j >= low_chunks, high_slot, low_slot))
        return slots

    top_low, top_high = tops[0], tops[1]
    rate = scale * LOG2_E
    stats[0] = jnp.max(top_low, axis=0, keepdims=True) * rate
    stats[1] = jnp.max(top_high, axis=0, keepdims=True) * rate

    def exponents(n, carry):
        part = jnp.exp2(scores[n] * rate - stats[1])
        scores[n] = part
        sums[n] = fold_rows(part, jnp.add)
        return carry

    lax.fori_loop(0, FIRST, exponents, 0)

    def other_exponents(j, carry):
        value = jnp.concatenate([other_scores[slot] for slot in other_slots(j)], axis=0)
        part = jnp.exp2(value * rate - stats[kind_of(j)])
        scores[FIRST + j] = part
        sums[FIRST + j] = fold_rows(part, jnp.add)
        return carry

    lax.fori_loop(0, OTHER, other_exponents, 0)

    sum_low = jnp.zeros((8, ROWS), f32)
    sum_high = jnp.zeros((8, ROWS), f32)
    for n in range(FIRST):
        sum_high = sum_high + sums[n]
    for j in range(OTHER):
        high = j >= low_chunks
        sum_low = sum_low + jnp.where(high, 0.0, sums[FIRST + j])
        sum_high = sum_high + jnp.where(high, sums[FIRST + j], 0.0)
    stats[0] = 1.0 / jnp.sum(sum_low, axis=0, keepdims=True)
    stats[1] = 1.0 / jnp.sum(sum_high, axis=0, keepdims=True)

    def chunk_grads(n, kind, chunk, d_part):
        expo = scores[n]
        inv_sum = stats[kind]
        prob = (expo * inv_sum).astype(bf16)
        d_score = ((d_part - delta[kind]) * (expo * (inv_sum * scale))).astype(bf16)
        dq = dot(d_score, chunk, 0, 0)
        dk = dot(d_score, queries[kind], 1, 0)
        dk_lat = dk[:, :LAT] + dot(prob, d_latent[kind], 1, 0)
        return dq, dk_lat, dk[:, LAT:]

    def other_grads(j, carry):
        d_part = jnp.concatenate([other_prob[slot] for slot in other_slots(j)], axis=0)
        dq, dk_lat, dk_rope = chunk_grads(FIRST + j, kind_of(j), other_keys(j), d_part)
        for i in range(4):
            rows = slice(i * SPAN, (i + 1) * SPAN)
            other_terms[4 * j + i, :, :LAT] = dk_lat[rows]
            other_terms[4 * j + i, :, LAT:] = dk_rope[rows]

        fresh = (j == 0) | (j == low_chunks)
        before = dq_prefix[jnp.maximum(j - 1, 0)]
        dq_prefix[j] = dq + jnp.where(fresh, 0.0, before)
        return carry

    dq_prefix[0] = jnp.zeros((ROWS, CAT), f32)
    lax.fori_loop(0, OTHER, other_grads, 0)

    def r_first(c):
        return HALF if c == 0 else HALF - 1

    def r_end(c):
        return 1 if c == 0 else 0

    def r_unit(c, k):
        return wrap(z + k, NZ) if c == 0 else wrap(z - k, NZ)

    def ra(c, k):
        return remote(terms.at[r_unit(c, k)], sib_in.at[k], ra_s.at[k], ra_r.at[k], sibling)

    def rl(c, k, j):
        unit = r_unit(c, k)
        if c == 0:
            ref, device = terms.at[unit, :, wrap(y + j, NP)], at_y(j)
        else:
            ref, device = terms.at[unit, wrap(x + j, NP)], at_x(j)
        return remote(ref, line_in.at[k, j - 1], rl_s.at[k, j], rl_r.at[k, j], device)

    def rp(c, k, j):
        unit = r_unit(c, k)
        if c == 0:
            ref, device = terms.at[unit, wrap(x + j, NP), y], at_x(j)
        else:
            ref, device = terms.at[unit, x, wrap(y + j, NP)], at_y(j)
        return remote(ref, piece_in.at[k, j - 1], rp_s.at[k, j], rp_r.at[k, j], device)

    def rz(c, k):
        unit = r_unit(c, k)
        device = {"ctx": unit * 2 + holder, "head": head}
        return remote(terms.at[unit, x, y], ring_in.at[c, k], rz_s.at[k], rz_r.at[c, k], device)

    def rw(c):
        unit = r_unit(c, 1)
        device = {"ctx": unit * 2 + 1, "head": head}
        return remote(terms.at[unit], whole_in.at[c], rw_s.at[0], rw_r.at[c], device)

    def first_grads(k):
        n = k - 1
        dq, dk_lat, dk_rope = chunk_grads(n, 1, first_keys(k), d_prob[n])
        dq_first[...] += dq
        units = (wrap(z - k, NZ), wrap(z + lax.rem(k, HALF), NZ))
        for s in range(2):
            unit = units[s]
            for cc in range(2):
                block = table[0, unit * 2 + cc]
                low_slot = jnp.where(block < 4 * low_chunks, block, BLANK)
                high_slot = jnp.minimum(4 * low_chunks + (2 * NZ - 1 - block), BLANK)
                low_term = other_terms[low_slot]
                rows = slice((2 * s + cc) * SPAN, (2 * s + cc + 1) * SPAN)
                terms[unit, cc, :, :, :LAT] = (
                    (dk_lat[rows] + low_term[:, :LAT]).astype(bf16).reshape(NP, PIECE, LAT)
                )
                terms[unit, cc, :, :, LAT:] = (
                    (dk_rope[rows] + low_term[:, LAT:]).astype(bf16).reshape(NP, PIECE, ROPE)
                )
                terms[unit, 2 + cc] = other_terms[high_slot].astype(bf16).reshape(NP, PIECE, CAT)

    def turn(i):
        return jnp.where(i == 0, 1, jnp.where(i == HALF, 0, HALF + 1 - i))

    def served(c, k):
        return (k >= r_end(c)) & (k <= r_first(c))

    def reduce_step(i):
        k = turn(i)

        @pl.when(i < HALF)
        def _():
            first_grads(k)

        def own(c):
            @pl.when((i <= HALF) & served(1 - c, k))
            def _():
                ra(1 - c, k).start()

            ka = turn(i - 1)

            @pl.when((i >= 1) & served(c, ka))
            def _():
                unit = r_unit(c, ka)
                ra(c, ka).wait_recv()
                both = terms[unit].astype(f32) + sib_in[ka].astype(f32)
                if c == 1:
                    added = ka == 0

                    @pl.when(added)
                    def _():
                        rw(0).wait_recv()
                        rw(1).wait_recv()
                        total = both + whole_in[0].astype(f32) + whole_in[1].astype(f32)
                        terms[unit] = total.astype(bf16)

                    @pl.when(jnp.logical_not(added))
                    def _():
                        terms[unit] = both.astype(bf16)

                else:
                    terms[unit] = both.astype(bf16)

                @pl.when(ka == 1)
                def _():
                    rw(c).start()

                @pl.when(ka != 1)
                def _():
                    for j in (2, 1, 3):
                        rl(c, ka, j).start()

        by_core(own)

    each(0, HALF + 2, reduce_step)

    low = dq_prefix[low_chunks - 1]
    high = dq_prefix[OTHER - 1] + dq_first[...]
    for half, part in ((0, low), (1, high)):
        toks = slice(half * SPAN, (half + 1) * SPAN)
        dq_lat = part[:, :LAT].astype(bf16)
        dq_rope = part[:, LAT:]
        for h in range(HEADS):
            rows = slice(h * SPAN, (h + 1) * SPAN)
            dq_nope_out[toks, h * NOPE : (h + 1) * NOPE] = dot(
                dq_lat[rows], w_uk[h], 1, 1
            ).astype(bf16)
        for h in range(0, HEADS, 2):
            pair = jnp.concatenate(
                [dq_rope[h * SPAN : (h + 1) * SPAN], dq_rope[(h + 1) * SPAN : (h + 2) * SPAN]],
                axis=1,
            )
            dq_rope_out[toks, h * ROPE : (h + 2) * ROPE] = pair.astype(bf16)
    stores = [
        pltpu.make_async_copy(dq_nope_out, dq_nope_res, out_sem.at[0]),
        pltpu.make_async_copy(dq_rope_out, dq_rope_res, out_sem.at[1]),
    ]
    for store in stores:
        store.start()

    def sum_line(c, k):
        unit = r_unit(c, k)
        for j in (1, 2, 3):
            rl(c, k, j).wait_recv()
        total = terms[unit, :, y] if c == 0 else terms[unit, x]
        total = total.astype(f32)
        for j in range(3):
            total = total + line_in[k, j].astype(f32)
        if c == 0:
            terms[unit, :, y] = total.astype(bf16)
        else:
            terms[unit, x] = total.astype(bf16)
        for j in (2, 1, 3):
            rp(c, k, j).start()

    def sum_piece(c, k):
        unit = r_unit(c, k)
        for j in (1, 2, 3):
            rp(c, k, j).wait_recv()
        total = terms[unit, x, y].astype(f32)
        for j in range(3):
            total = total + piece_in[k, j].astype(f32)
        terms[unit, x, y] = total.astype(bf16)

        if c == 0:
            rz(c, k).start()
        else:
            kept = (k == 0) & holds

            @pl.when(kept)
            def _():
                ring_in[c, 0] = terms[unit, x, y]

            @pl.when(jnp.logical_not(kept))
            def _():
                rz(c, k).start()

    def plane_turn(i):
        return jnp.where(i == HALF - 1, 0, HALF - i)

    def sum_over_plane(c):
        def step(i):
            k = plane_turn(i)

            @pl.when((i < HALF) & served(c, k))
            def _():
                sum_line(c, k)

            late = plane_turn(i - LAG_R)

            @pl.when((i >= LAG_R) & served(c, late))
            def _():
                sum_piece(c, late)

        each(0, HALF + LAG_R, step)

    by_core(sum_over_plane)

    def f1(i, j, back):
        if back:
            xs, ys = wrap(x - i, NP), wrap(y - j, NP)
        else:
            xs, ys = x, y
        ref = result.at[lax.div(xs, 2), ys]
        return remote(ref, ref, f1_s.at[i, j], f1_r.at[i, j], at_plane(i, j))

    far_first = sorted(
        ((i, j) for i in range(NP) for j in range(NP) if i or j),
        key=lambda ij: -(min(ij[0], NP - ij[0]) + min(ij[1], NP - ij[1])),
    )

    @pl.when(holds)
    def _():
        share[...] = jnp.zeros((PIECE, CAT), f32)
        for c in range(2):

            def step(i, c=c):
                k = plane_turn(i)

                @pl.when(served(c, k))
                def _():
                    @pl.when(jnp.logical_not((k == 0) & (core == 1)))
                    def _():
                        rz(c, k).wait_recv()

                    share[...] += ring_in[c, k].astype(f32)

            each(0, HALF, step)
        result[lax.div(x, 2), y] = share[...].astype(bf16)
        for i, j in far_first:
            f1(i, j, False).start()

    for i, j in reversed(far_first):

        @pl.when(lax.rem(x + NP - i, 2) == core)
        def _():
            f1(i, j, True).wait_recv()

    gain_row = gain[...].reshape(1, LAT).astype(f32)
    kv_rows = kv_t[...].T
    grads = result[...].reshape(2 * SPAN, CAT).astype(f32)
    values = kv_rows[:, :LAT].astype(f32)
    inv = lax.rsqrt(jnp.mean(values * values, axis=-1, keepdims=True) + EPS_NORM)
    scaled = grads[:, :LAT] * gain_row
    inner = jnp.mean(values * scaled, axis=-1, keepdims=True)
    d_raw = inv * scaled - values * (inv * inv * inv * inner)
    d_cache_out[:LAT, :] = d_raw.T
    d_cache_out[LAT:, :] = grads[:, LAT:].T
    store = pltpu.make_async_copy(d_cache_out, d_cache_res, out_sem.at[2])
    store.start()

    for n in range(2):
        g_own(n).wait_send()

    def sends(c):
        def gather_step(d):
            @pl.when(d <= NEAR)
            def _():
                gz(c, d, z, "line").wait_send()

            @pl.when(d > NEAR)
            def _():
                gz(c, d, z).wait_send()
                for j in (1, 2, 3):
                    gp(c, d, j, 0).wait_send()

            for j in (1, 2, 3):
                gl(c, d, j, 0).wait_send()
            gs(c, d).wait_send()

        gz(c, 1, z, "unit").wait_send()
        gs(c, 1).wait_send()

        each(2, g_last(c) + 1, gather_step)

        def reduce_twin(k):
            ra(1 - c, k).wait_send()

        each(r_end(1 - c), r_first(1 - c) + 1, reduce_twin)

        def reduce_sends(k):
            for j in (1, 2, 3):
                rl(c, k, j).wait_send()
                rp(c, k, j).wait_send()

        rw(c).wait_send()
        if c == 1:
            reduce_sends(0)
        each(2, r_first(c) + 1, reduce_sends)
        each(2, r_first(c) + 1, lambda k: rz(c, k).wait_send())
        if c == 1:

            @pl.when(jnp.logical_not(holds))
            def _():
                rz(c, 0).wait_send()

    by_core(sends)

    @pl.when(holds)
    def _():
        for i, j in far_first:
            f1(i, j, False).wait_send()

    for done in stores:
        done.wait()
    store.wait()


def hand_over(*refs):
    for src, dst in zip(refs[:3], refs[3:]):
        dst[...] = src[...]


def local(q_nope, q_rope, kv_cache, kv_gain, w_uk, w_uv, attn_out, d_out, span_table):
    toks = q_nope.shape[0]
    hbm = pl.BlockSpec(memory_space=pl.ANY)
    smem = pl.BlockSpec(memory_space=pltpu.SMEM)
    vmem = pl.BlockSpec(memory_space=pltpu.VMEM)
    dma = pltpu.SemaphoreType.DMA
    inputs = (
        q_nope, q_rope, kv_cache.T, kv_gain, w_uk, w_uv, attn_out, d_out
    )
    out_shape = (
        jax.ShapeDtypeStruct((toks, HEADS * NOPE), bf16),
        jax.ShapeDtypeStruct((toks, HEADS * ROPE), bf16),
        jax.ShapeDtypeStruct((CAT, toks), f32),
    )
    scratch = [pltpu.VMEM(value.shape, value.dtype) for value in inputs]
    scratch += [pltpu.VMEM(value.shape, value.dtype) for value in out_shape]
    scratch += [
        pltpu.VMEM((NZ, NP, NP, PIECE, CAT), bf16),
        pltpu.VMEM((NZ, NP, NP, PIECE, CAT), bf16),
        pltpu.VMEM((HALF + 1, NP, NP, PIECE, CAT), bf16),
        pltpu.VMEM((HALF + 1, 3, NP, PIECE, CAT), bf16),
        pltpu.VMEM((HALF + 1, 3, PIECE, CAT), bf16),
        pltpu.VMEM((2, HALF + 1, PIECE, CAT), bf16),
        pltpu.VMEM((2, NP, NP, PIECE, CAT), bf16),
        pltpu.VMEM((PIECE, CAT), f32),
        pltpu.VMEM((2, NP, PIECE, CAT), bf16),
        pltpu.VMEM((2, ROWS, CAT), bf16),
        pltpu.VMEM((2, ROWS, LAT), bf16),
        pltpu.VMEM((2, 1, ROWS), f32),
        pltpu.VMEM((FIRST + OTHER, CHUNK, ROWS), f32),
        pltpu.VMEM((FIRST, CHUNK, ROWS), f32),
        pltpu.VMEM((HIDDEN + 1, SPAN, ROWS), f32),
        pltpu.VMEM((HIDDEN + 1, SPAN, ROWS), f32),
        pltpu.VMEM((2, 8, ROWS), f32),
        pltpu.VMEM((BLANK + 1, SPAN, CAT), f32),
        pltpu.VMEM((OTHER, ROWS, CAT), f32),
        pltpu.VMEM((ROWS, CAT), f32),
        pltpu.VMEM((2, 1, ROWS), f32),
        pltpu.VMEM((FIRST + OTHER, 8, ROWS), f32),
        pltpu.SMEM((2 * NZ,), jnp.int32),
        dma((len(inputs),)),
        dma((3,)),
        dma((2,)), dma((2,)),
        dma((HALF + 1,)), dma((HALF + 1,)),
        dma((HALF + 1, NP)), dma((HALF + 1, NP)),
        dma((HALF + 1, NP)), dma((HALF + 1, NP)),
        dma((HALF + 1,)), dma((HALF + 1,)),
        dma((HALF + 1,)), dma((HALF + 1,)),
        dma((HALF + 1, NP)), dma((HALF + 1, NP)),
        dma((HALF + 1, NP)), dma((HALF + 1, NP)),
        dma((HALF + 1,)), dma((2, HALF + 1)),
        dma((1,)), dma((2,)),
        dma((NP, NP)), dma((NP, NP)),
    ]
    results = pl.pallas_call(
        kernel,
        out_shape=out_shape,
        in_specs=[hbm] * len(inputs) + [smem],
        out_specs=(hbm, hbm, hbm),
        scratch_shapes=scratch,
        compiler_params=pltpu.CompilerParams(
            collective_id=0, has_side_effects=True, vmem_limit_bytes=60 * 1024 * 1024
        ),
    )(*inputs, span_table.T)
    d_q_nope, d_q_rope, d_cache = pl.pallas_call(
        hand_over,
        out_shape=out_shape,
        in_specs=[vmem] * 3,
        out_specs=(vmem, vmem, vmem),
        compiler_params=pltpu.CompilerParams(vmem_limit_bytes=60 * 1024 * 1024),
    )(*results)
    return d_q_nope, d_q_rope, d_cache.T


def solution(mesh):
    in_specs = (
        P("ctx", "head"),
        P("ctx", "head"),
        P("ctx", None),
        P(),
        P("head", None, None),
        P("head", None, None),
        P("ctx", "head"),
        P("ctx", "head"),
        P(),
    )
    out_specs = (P("ctx", "head"), P("ctx", "head"), P("ctx", None))
    return jax.shard_map(local, mesh=mesh, in_specs=in_specs, out_specs=out_specs, check_vma=False)
```

```python
import functools

import jax
import jax.numpy as jnp
from jax import lax
from jax.experimental import pallas as pl
from jax.experimental.pallas import tpu as pltpu
from jax.sharding import PartitionSpec as P

MESH = pl.DeviceIdType.MESH
NEG_BIG = -1e30
EPS_NORM = 1e-06
LOG2_E = 1.4426950408889634

NZ = 16
HALF = NZ // 2
NP = 4
PIECE = 16
SPAN = 64
HEADS = 4
ROWS = SPAN * HEADS
LAT = 512
ROPE = 64
LAG_G = 4
NEAR = 2
LAG_R = 2
CAT = LAT + ROPE
NOPE = 128
CHUNK = 256
FIRST = 8
OTHER = 9
OWN_LOW = 2 * NZ
HIDDEN = OWN_LOW + 1
BLANK = 4 * OTHER

f32 = jnp.float32
bf16 = jnp.bfloat16


def dot(a, b, ca, cb):
    return lax.dot_general(a, b, (((ca,), (cb,)), ((), ())), preferred_element_type=f32)


def wrap(value, size):
    return lax.rem(value + 2 * size, size)


def kernel(
    q_nope_in, q_rope_in, kv_in, gain_in, w_uk_in, w_uv_in, attn_out_in, d_out_in, table,
    dq_nope_res, dq_rope_res, d_cache_res,
    q_nope, q_rope, kv_t, gain, w_uk, w_uv, attn_out, d_out,
    dq_nope_out, dq_rope_out, d_cache_out,
    keys, terms, sib_in, line_in, piece_in, ring_in, whole_in, share, result,
    queries, d_latent, delta, scores, d_prob, other_scores, other_prob, tops, other_terms, dq_prefix, dq_first,
    stats, sums, values_ref, inv_ref, inverse, in_sem, out_sem,
    g0_s, g0_r, gz_s, gz_r, gp_s, gp_r, gl_s, gl_r, gs_s, gs_r,
    ra_s, ra_r, rl_s, rl_r, rp_s, rp_r, rz_s, rz_r, rw_s, rw_r, f1_s, f1_r,
):
    scale = float(NOPE + ROPE) ** (-0.5)
    ctx = lax.axis_index("ctx")
    head = lax.axis_index("head")
    z, core = lax.div(ctx, 2), lax.rem(ctx, 2)
    x, y = lax.div(head, NP), lax.rem(head, NP)
    twin = 1 - core

    def at_x(j):
        return {"ctx": ctx, "head": wrap(x + j, NP) * NP + y}

    def at_y(j):
        return {"ctx": ctx, "head": x * NP + wrap(y + j, NP)}

    def at_z(zz):
        return {"ctx": zz * 2 + core, "head": head}

    sibling = {"ctx": z * 2 + twin, "head": head}

    def remote(src, dst, send, recv, device):
        return pltpu.make_async_remote_copy(
            src_ref=src, dst_ref=dst, send_sem=send, recv_sem=recv,
            device_id=device, device_id_type=MESH,
        )

    def by_core(step):
        for c in range(2):
            pl.when(core == c)(functools.partial(step, c))

    holds = lax.rem(x, 2) == core
    holder = lax.rem(x, 2)

    def at_plane(i, j):
        return {"ctx": ctx, "head": wrap(x + i, NP) * NP + wrap(y + j, NP)}

    barrier = pltpu.get_barrier_semaphore()

    def signal(device):
        pl.semaphore_signal(barrier, inc=1, device_id=device, device_id_type=MESH)

    def greet(c):
        for d in range(HALF if c == 0 else HALF - 1, 0, -1):
            signal({"ctx": wrap(z - d if c == 0 else z + d, NZ) * 2 + c, "head": head})
        if c == 1:
            signal({"ctx": wrap(z - 1, NZ) * 2, "head": head})

        @pl.when(holds)
        def _():
            for d in range(HALF - 1 if c == 0 else HALF, 1, -1):
                signal({"ctx": wrap(z + d if c == 0 else z - d, NZ) * 2 + 1 - c, "head": head})

    by_core(greet)
    for i in range(NP):
        for j in range(NP):
            if i and j:

                @pl.when(lax.rem(x + i, 2) == core)
                def _():
                    signal(at_plane(i, j))

            elif i or j:
                signal(at_plane(i, j))
    signal(sibling)

    loads = [
        pltpu.make_async_copy(src, dst, in_sem.at[n])
        for n, (src, dst) in enumerate(
            (
                (kv_in, kv_t), (gain_in, gain), (q_nope_in, q_nope), (w_uk_in, w_uk),
                (q_rope_in, q_rope), (d_out_in, d_out), (w_uv_in, w_uv), (attn_out_in, attn_out),
            )
        )
    ]
    for load in loads:
        load.start()

    loads[0].wait()
    loads[1].wait()
    kv = kv_t[...].T
    raw = kv[:, :LAT].astype(f32)
    inv_norm = lax.rsqrt(jnp.mean(raw * raw, axis=-1, keepdims=True) + EPS_NORM)
    latent = (raw * inv_norm * gain[...].reshape(1, LAT).astype(f32)).astype(bf16)
    own_rope = kv[:, LAT:]
    for half in range(2):
        rows = slice(half * SPAN, (half + 1) * SPAN)
        keys[z, 2 * half + core, :, :, :LAT] = latent[rows].reshape(NP, PIECE, LAT)
        keys[z, 2 * half + core, :, :, LAT:] = own_rope[rows].reshape(NP, PIECE, ROPE)

    for load in loads[2:]:
        load.wait()
    for h in range(HEADS):
        cols = slice(h * NOPE, (h + 1) * NOPE)
        rows = slice(h * SPAN, (h + 1) * SPAN)
        q_lat = dot(q_nope[:, cols], w_uk[h], 1, 0).astype(bf16)
        d_lat = dot(d_out[:, cols], w_uv[h], 1, 1).astype(bf16)
        for half in range(2):
            toks = slice(half * SPAN, (half + 1) * SPAN)
            queries[half, rows, :LAT] = q_lat[toks]
            queries[half, rows, LAT:] = q_rope[toks, h * ROPE : (h + 1) * ROPE]
            d_latent[half, rows, :] = d_lat[toks]
    for half in range(2):
        toks = slice(half * SPAN, (half + 1) * SPAN)
        prods = [
            d_out[toks, h * NOPE : (h + 1) * NOPE].astype(f32)
            * attn_out[toks, h * NOPE : (h + 1) * NOPE].astype(f32)
            for h in range(HEADS)
        ]
        prod = jnp.concatenate(prods, axis=0)
        delta[half] = jnp.sum(prod.T, axis=0, keepdims=True)

    tops[...] = jnp.full(tops.shape, NEG_BIG, f32)
    dq_first[...] = jnp.zeros(dq_first.shape, f32)
    other_terms[BLANK] = jnp.zeros((SPAN, CAT), f32)
    other_scores[HIDDEN] = jnp.full((SPAN, ROWS), NEG_BIG, f32)
    other_prob[HIDDEN] = jnp.zeros((SPAN, ROWS), f32)

    targets = 2 * (NP - 1) + 1
    held = targets + (NP - 1) ** 2 + (HALF + 1) - 2 * core
    given = targets + 2 * HALF - 3 * core
    pl.semaphore_wait(barrier, jnp.where(holds, held, given))

    def g_last(c):
        return HALF if c == 0 else HALF - 1

    def g_unit(c, d):
        return wrap(z - d, NZ) if c == 0 else wrap(z + d, NZ)

    def g_own(n):
        ref = keys.at[z, 2 * n + core]
        return remote(ref, ref, g0_s.at[n], g0_r.at[n], sibling)

    def g_own_arrival(n):
        ref = keys.at[z, 2 * n + twin]
        return remote(ref, ref, g0_s.at[n], g0_r.at[n], sibling)

    def gz(c, d, unit, form="piece"):
        if form == "unit":
            ref = keys.at[unit]
        elif form == "line":
            ref = keys.at[unit, :, y] if c == 0 else keys.at[unit, x]
        else:
            ref = keys.at[unit, x, y]
        device = at_z(wrap(z + d, NZ) if c == 0 else wrap(z - d, NZ))
        return remote(ref, ref, gz_s.at[d], gz_r.at[d], device)

    def gp(c, d, j, back):
        unit = g_unit(c, d)
        if c == 0:
            ref, device = keys.at[unit, wrap(x - back, NP), y], at_x(j)
        else:
            ref, device = keys.at[unit, x, wrap(y - back, NP)], at_y(j)
        return remote(ref, ref, gp_s.at[d, j], gp_r.at[d, j], device)

    def gl(c, d, j, back):
        unit = g_unit(c, d)
        if c == 0:
            ref, device = keys.at[unit, :, wrap(y - back, NP)], at_y(j)
        else:
            ref, device = keys.at[unit, wrap(x - back, NP)], at_x(j)
        return remote(ref, ref, gl_s.at[d, j], gl_r.at[d, j], device)

    def gs(c, d):
        ref = keys.at[g_unit(c, d)]
        return remote(ref, ref, gs_s.at[d], gs_r.at[d], sibling)

    for n in range(2):
        g_own(n).start()
    for n in range(2):
        g_own_arrival(n).wait_recv()

    def each(low, high, step):
        def body(d, carry):
            step(d)
            return carry

        lax.fori_loop(low, high, body, 0)

    def spread_z(c):
        each(NEAR + 1, g_last(c) + 1, lambda d: gz(c, g_last(c) + NEAR + 1 - d, z).start())
        each(2, NEAR + 1, lambda d: gz(c, d, z, "line").start())
        gz(c, 1, z, "unit").start()

    by_core(spread_z)

    def invert(b, carry):
        found = jnp.int32(0)
        for d in range(2 * NZ):
            found = found + jnp.where(table[0, d] == b, d, 0)
        inverse[b] = jnp.minimum(found, 2 * NZ - 1)
        return carry

    lax.fori_loop(0, 2 * NZ, invert, 0)
    mine = table[0, ctx]
    low_chunks = lax.div(mine + 4, 4)

    def spread(c):
        def near_step(d):
            gz(c, d, g_unit(c, d), "line").wait_recv()
            for j in (2, 1, 3):
                gl(c, d, j, 0).start()

        each(2, NEAR + 1, near_step)

        def step(d):
            @pl.when(d <= g_last(c))
            def _():
                gz(c, d, g_unit(c, d)).wait_recv()
                for j in (2, 1, 3):
                    gp(c, d, j, 0).start()

            e = d - LAG_G

            @pl.when(e >= NEAR + 1)
            def _():
                for j in (1, 2, 3):
                    gp(c, e, j, j).wait_recv()
                for j in (2, 1, 3):
                    gl(c, e, j, 0).start()

        each(NEAR + 1, g_last(c) + LAG_G + 1, step)

    by_core(spread)

    def first_keys(t):
        low = keys[wrap(z - t, NZ), 0:2].reshape(CHUNK // 2, CAT)
        high = keys[wrap(z + lax.rem(t, HALF), NZ), 0:2].reshape(CHUNK // 2, CAT)
        return jnp.concatenate([low, high], axis=0)

    def fold_rows(value, op):
        part = value[0:8]
        for r in range(8, value.shape[0], 8):
            part = op(part, value[r : r + 8])
        return part

    key_in = lax.broadcasted_iota(jnp.int32, (SPAN, ROWS), 0)
    tok_in = lax.rem(lax.broadcasted_iota(jnp.int32, (SPAN, ROWS), 1), SPAN)

    own_low = keys[z, core].reshape(SPAN, CAT)
    own_part = jnp.where(key_in <= tok_in, dot(own_low, queries[0], 1, 1), NEG_BIG)
    other_scores[OWN_LOW] = own_part
    other_prob[OWN_LOW] = dot(own_low[:, :LAT], d_latent[0], 1, 1)
    tops[0] = fold_rows(own_part, jnp.maximum)

    def arrivals(d):
        def own(c):
            @pl.when(d == 1)
            def _():
                gz(c, 1, g_unit(c, 1), "unit").wait_recv()

            @pl.when((d >= 2) & (d <= g_last(c)))
            def _():
                for j in (1, 2, 3):
                    gl(c, d, j, j).wait_recv()

            @pl.when(d <= g_last(c))
            def _():
                gs(c, d).start()

            @pl.when((d >= 2) & (d - 1 <= g_last(1 - c)))
            def _():
                gs(1 - c, d - 1).wait_recv()

        by_core(own)

        @pl.when(d >= 2)
        def _():
            t = d - 1
            chunk = first_keys(t)
            part = dot(chunk, queries[1], 1, 1)
            scores[t - 1] = part
            tops[1] = jnp.maximum(tops[1], fold_rows(part, jnp.maximum))
            d_prob[t - 1] = dot(chunk[:, :LAT], d_latent[1], 1, 1)

            slots, kinds, blocks = [], [], []
            for unit in (wrap(z - t, NZ), wrap(z + lax.rem(t, HALF), NZ)):
                for cc in range(2):
                    slot = unit * 2 + cc
                    kind = jnp.where(table[0, slot] >= mine, 1, 0)
                    slots.append(slot)
                    kinds.append(kind)
                    block = jnp.where(kind == 1, keys[unit, 2 + cc], keys[unit, cc])
                    blocks.append(block.reshape(SPAN, CAT))
            chunk = jnp.concatenate(blocks, axis=0)
            part = [dot(chunk, queries[kind], 1, 1) for kind in range(2)]
            d_part = [dot(chunk[:, :LAT], d_latent[kind], 1, 1) for kind in range(2)]
            for n in range(4):
                rows = slice(n * SPAN, (n + 1) * SPAN)
                high = kinds[n] == 1
                block = jnp.where(high, part[1][rows], part[0][rows])
                gap = jnp.where(slots[n] == ctx, 0, -SPAN)
                block = jnp.where(key_in + gap <= tok_in, block, NEG_BIG)
                other_scores[slots[n]] = block
                other_prob[slots[n]] = jnp.where(high, d_part[1][rows], d_part[0][rows])
                top = fold_rows(block, jnp.maximum)
                tops[0] = jnp.maximum(tops[0], jnp.where(high, NEG_BIG, top))
                tops[1] = jnp.maximum(tops[1], jnp.where(high, top, NEG_BIG))

    each(1, HALF + 2, arrivals)

    def kind_of(j):
        return jnp.where(j >= low_chunks, 1, 0)

    def other_keys(j):
        kind = kind_of(j)
        blocks = []
        for i in range(4):
            low_id = inverse[jnp.minimum(4 * j + i, 2 * NZ - 1)]
            high_id = inverse[jnp.clip(2 * NZ - 1 - (4 * (j - low_chunks) + i), 0, 2 * NZ - 1)]
            owner = jnp.where(kind == 1, high_id, low_id)
            block = keys[lax.div(owner, 2), 2 * kind + lax.rem(owner, 2)]
            blocks.append(block.reshape(SPAN, CAT))
        return jnp.concatenate(blocks, axis=0)

    def other_slots(j):
        slots = []
        for i in range(4):
            low = 4 * j + i
            low_slot = inverse[jnp.minimum(low, 2 * NZ - 1)]
            low_slot = jnp.where(low < mine, low_slot, jnp.where(low == mine, OWN_LOW, HIDDEN))
            high = 2 * NZ - 1 - (4 * (j - low_chunks) + i)
            high_slot = inverse[jnp.clip(high, 0, 2 * NZ - 1)]
            high_slot = jnp.where(high >= mine, high_slot, HIDDEN)
            slots.append(jnp.where(j >= low_chunks, high_slot, low_slot))
        return slots

    top_low, top_high = tops[0], tops[1]
    rate = scale * LOG2_E
    stats[0] = jnp.max(top_low, axis=0, keepdims=True) * rate
    stats[1] = jnp.max(top_high, axis=0, keepdims=True) * rate

    def exponents(n, carry):
        part = jnp.exp2(scores[n] * rate - stats[1])
        scores[n] = part
        sums[n] = fold_rows(part, jnp.add)
        return carry

    lax.fori_loop(0, FIRST, exponents, 0)

    def other_exponents(j, carry):
        value = jnp.concatenate([other_scores[slot] for slot in other_slots(j)], axis=0)
        part = jnp.exp2(value * rate - stats[kind_of(j)])
        scores[FIRST + j] = part
        sums[FIRST + j] = fold_rows(part, jnp.add)
        return carry

    lax.fori_loop(0, OTHER, other_exponents, 0)

    sum_low = jnp.zeros((8, ROWS), f32)
    sum_high = jnp.zeros((8, ROWS), f32)
    for n in range(FIRST):
        sum_high = sum_high + sums[n]
    for j in range(OTHER):
        high = j >= low_chunks
        sum_low = sum_low + jnp.where(high, 0.0, sums[FIRST + j])
        sum_high = sum_high + jnp.where(high, sums[FIRST + j], 0.0)
    stats[0] = 1.0 / jnp.sum(sum_low, axis=0, keepdims=True)
    stats[1] = 1.0 / jnp.sum(sum_high, axis=0, keepdims=True)

    def chunk_grads(n, kind, chunk, d_part):
        expo = scores[n]
        inv_sum = stats[kind]
        prob = (expo * inv_sum).astype(bf16)
        d_score = ((d_part - delta[kind]) * (expo * (inv_sum * scale))).astype(bf16)
        dq = dot(d_score, chunk, 0, 0)
        dk = dot(d_score, queries[kind], 1, 0)
        dk_lat = dk[:, :LAT] + dot(prob, d_latent[kind], 1, 0)
        return dq, dk_lat, dk[:, LAT:]

    def other_grads(j, carry):
        d_part = jnp.concatenate([other_prob[slot] for slot in other_slots(j)], axis=0)
        dq, dk_lat, dk_rope = chunk_grads(FIRST + j, kind_of(j), other_keys(j), d_part)
        for i in range(4):
            rows = slice(i * SPAN, (i + 1) * SPAN)
            other_terms[4 * j + i, :, :LAT] = dk_lat[rows]
            other_terms[4 * j + i, :, LAT:] = dk_rope[rows]

        fresh = (j == 0) | (j == low_chunks)
        before = dq_prefix[jnp.maximum(j - 1, 0)]
        dq_prefix[j] = dq + jnp.where(fresh, 0.0, before)
        return carry

    dq_prefix[0] = jnp.zeros((ROWS, CAT), f32)
    lax.fori_loop(0, OTHER, other_grads, 0)

    def r_first(c):
        return HALF if c == 0 else HALF - 1

    def r_end(c):
        return 1 if c == 0 else 0

    def r_unit(c, k):
        return wrap(z + k, NZ) if c == 0 else wrap(z - k, NZ)

    def ra(c, k):
        return remote(terms.at[r_unit(c, k)], sib_in.at[k], ra_s.at[k], ra_r.at[k], sibling)

    def rl(c, k, j):
        unit = r_unit(c, k)
        if c == 0:
            ref, device = terms.at[unit, :, wrap(y + j, NP)], at_y(j)
        else:
            ref, device = terms.at[unit, wrap(x + j, NP)], at_x(j)
        return remote(ref, line_in.at[k, j - 1], rl_s.at[k, j], rl_r.at[k, j], device)

    def rp(c, k, j):
        unit = r_unit(c, k)
        if c == 0:
            ref, device = terms.at[unit, wrap(x + j, NP), y], at_x(j)
        else:
            ref, device = terms.at[unit, x, wrap(y + j, NP)], at_y(j)
        return remote(ref, piece_in.at[k, j - 1], rp_s.at[k, j], rp_r.at[k, j], device)

    def rz(c, k):
        unit = r_unit(c, k)
        device = {"ctx": unit * 2 + holder, "head": head}
        return remote(terms.at[unit, x, y], ring_in.at[c, k], rz_s.at[k], rz_r.at[c, k], device)

    def rw(c):
        unit = r_unit(c, 1)
        device = {"ctx": unit * 2 + 1, "head": head}
        return remote(terms.at[unit], whole_in.at[c], rw_s.at[0], rw_r.at[c], device)

    def first_grads(k):
        n = k - 1
        dq, dk_lat, dk_rope = chunk_grads(n, 1, first_keys(k), d_prob[n])
        dq_first[...] += dq
        units = (wrap(z - k, NZ), wrap(z + lax.rem(k, HALF), NZ))
        for s in range(2):
            unit = units[s]
            for cc in range(2):
                block = table[0, unit * 2 + cc]
                low_slot = jnp.where(block < 4 * low_chunks, block, BLANK)
                high_slot = jnp.minimum(4 * low_chunks + (2 * NZ - 1 - block), BLANK)
                low_term = other_terms[low_slot]
                rows = slice((2 * s + cc) * SPAN, (2 * s + cc + 1) * SPAN)
                terms[unit, cc, :, :, :LAT] = (
                    (dk_lat[rows] + low_term[:, :LAT]).astype(bf16).reshape(NP, PIECE, LAT)
                )
                terms[unit, cc, :, :, LAT:] = (
                    (dk_rope[rows] + low_term[:, LAT:]).astype(bf16).reshape(NP, PIECE, ROPE)
                )
                terms[unit, 2 + cc] = other_terms[high_slot].astype(bf16).reshape(NP, PIECE, CAT)

    def turn(i):
        later = jnp.where(i == HALF, 0, HALF + 1 - i)
        return jnp.where(i == 0, HALF, jnp.where(i == 1, 1, later))

    def served(c, k):
        return (k >= r_end(c)) & (k <= r_first(c))

    def reduce_step(i):
        k = turn(i)

        @pl.when(i < HALF)
        def _():
            first_grads(k)

        def own(c):
            @pl.when((i <= HALF) & served(1 - c, k))
            def _():
                ra(1 - c, k).start()

            ka = turn(i - 1)

            @pl.when((i >= 1) & served(c, ka))
            def _():
                unit = r_unit(c, ka)
                ra(c, ka).wait_recv()
                both = terms[unit].astype(f32) + sib_in[ka].astype(f32)
                if c == 1:
                    added = ka == 0

                    @pl.when(added)
                    def _():
                        rw(0).wait_recv()
                        rw(1).wait_recv()
                        total = both + whole_in[0].astype(f32) + whole_in[1].astype(f32)
                        terms[unit] = total.astype(bf16)

                    @pl.when(jnp.logical_not(added))
                    def _():
                        terms[unit] = both.astype(bf16)

                else:
                    terms[unit] = both.astype(bf16)

                @pl.when(ka == 1)
                def _():
                    rw(c).start()

                @pl.when(ka != 1)
                def _():
                    for j in (2, 1, 3):
                        rl(c, ka, j).start()

        by_core(own)

    each(0, HALF + 2, reduce_step)

    low = dq_prefix[low_chunks - 1]
    high = dq_prefix[OTHER - 1] + dq_first[...]
    for half, part in ((0, low), (1, high)):
        toks = slice(half * SPAN, (half + 1) * SPAN)
        dq_lat = part[:, :LAT].astype(bf16)
        dq_rope = part[:, LAT:]
        for h in range(HEADS):
            rows = slice(h * SPAN, (h + 1) * SPAN)
            dq_nope_out[toks, h * NOPE : (h + 1) * NOPE] = dot(
                dq_lat[rows], w_uk[h], 1, 1
            ).astype(bf16)
        for h in range(0, HEADS, 2):
            pair = jnp.concatenate(
                [dq_rope[h * SPAN : (h + 1) * SPAN], dq_rope[(h + 1) * SPAN : (h + 2) * SPAN]],
                axis=1,
            )
            dq_rope_out[toks, h * ROPE : (h + 2) * ROPE] = pair.astype(bf16)
    stores = [
        pltpu.make_async_copy(dq_nope_out, dq_nope_res, out_sem.at[0]),
        pltpu.make_async_copy(dq_rope_out, dq_rope_res, out_sem.at[1]),
    ]
    for store in stores:
        store.start()

    gain_row = gain[...].reshape(1, LAT).astype(f32)
    own_rows = kv_t[...].T[:, :LAT].astype(f32)
    values_ref[...] = own_rows
    inv_ref[...] = lax.rsqrt(jnp.mean(own_rows * own_rows, axis=-1, keepdims=True) + EPS_NORM)

    def sum_line(c, k):
        unit = r_unit(c, k)
        for j in (1, 2, 3):
            rl(c, k, j).wait_recv()
        total = terms[unit, :, y] if c == 0 else terms[unit, x]
        total = total.astype(f32)
        for j in range(3):
            total = total + line_in[k, j].astype(f32)
        if c == 0:
            terms[unit, :, y] = total.astype(bf16)
        else:
            terms[unit, x] = total.astype(bf16)
        for j in (2, 1, 3):
            rp(c, k, j).start()

    def sum_piece(c, k):
        unit = r_unit(c, k)
        for j in (1, 2, 3):
            rp(c, k, j).wait_recv()
        total = terms[unit, x, y].astype(f32)
        for j in range(3):
            total = total + piece_in[k, j].astype(f32)
        terms[unit, x, y] = total.astype(bf16)

        if c == 0:
            rz(c, k).start()
        else:
            kept = (k == 0) & holds

            @pl.when(kept)
            def _():
                ring_in[c, 0] = terms[unit, x, y]

            @pl.when(jnp.logical_not(kept))
            def _():
                rz(c, k).start()

    def plane_turn(i):
        return jnp.where(i == HALF - 1, 0, HALF - i)

    def sum_over_plane(c):
        def step(i):
            k = plane_turn(i)

            @pl.when((i < HALF) & served(c, k))
            def _():
                sum_line(c, k)

            late = plane_turn(i - LAG_R)

            @pl.when((i >= LAG_R) & served(c, late))
            def _():
                sum_piece(c, late)

        each(0, HALF + LAG_R, step)

    by_core(sum_over_plane)

    def f1(i, j, back):
        if back:
            xs, ys = wrap(x - i, NP), wrap(y - j, NP)
        else:
            xs, ys = x, y
        ref = result.at[lax.div(xs, 2), ys]
        return remote(ref, ref, f1_s.at[i, j], f1_r.at[i, j], at_plane(i, j))

    far_first = sorted(
        ((i, j) for i in range(NP) for j in range(NP) if i or j),
        key=lambda ij: -(min(ij[0], NP - ij[0]) + min(ij[1], NP - ij[1])),
    )

    @pl.when(holds)
    def _():
        share[...] = jnp.zeros((PIECE, CAT), f32)
        for c in range(2):

            def step(i, c=c):
                k = plane_turn(i)

                @pl.when(served(c, k))
                def _():
                    @pl.when(jnp.logical_not((k == 0) & (core == 1)))
                    def _():
                        rz(c, k).wait_recv()

                    share[...] += ring_in[c, k].astype(f32)

            each(0, HALF, step)
        result[lax.div(x, 2), y] = share[...].astype(bf16)
        for i, j in far_first:
            f1(i, j, False).start()

    for i, j in reversed(far_first):

        @pl.when(lax.rem(x + NP - i, 2) == core)
        def _():
            f1(i, j, True).wait_recv()

    grads = result[...].reshape(2 * SPAN, CAT).astype(f32)
    values = values_ref[...]
    inv = inv_ref[...]
    scaled = grads[:, :LAT] * gain_row
    inner = jnp.mean(values * scaled, axis=-1, keepdims=True)
    d_raw = inv * scaled - values * (inv * inv * inv * inner)
    d_cache_out[:LAT, :] = d_raw.T
    d_cache_out[LAT:, :] = grads[:, LAT:].T
    store = pltpu.make_async_copy(d_cache_out, d_cache_res, out_sem.at[2])
    store.start()

    for n in range(2):
        g_own(n).wait_send()

    def sends(c):
        def gather_step(d):
            @pl.when(d <= NEAR)
            def _():
                gz(c, d, z, "line").wait_send()

            @pl.when(d > NEAR)
            def _():
                gz(c, d, z).wait_send()
                for j in (1, 2, 3):
                    gp(c, d, j, 0).wait_send()

            for j in (1, 2, 3):
                gl(c, d, j, 0).wait_send()
            gs(c, d).wait_send()

        gz(c, 1, z, "unit").wait_send()
        gs(c, 1).wait_send()

        each(2, g_last(c) + 1, gather_step)

        def reduce_twin(k):
            ra(1 - c, k).wait_send()

        each(r_end(1 - c), r_first(1 - c) + 1, reduce_twin)

        def reduce_sends(k):
            for j in (1, 2, 3):
                rl(c, k, j).wait_send()
                rp(c, k, j).wait_send()

        rw(c).wait_send()
        if c == 1:
            reduce_sends(0)
        each(2, r_first(c) + 1, reduce_sends)
        each(2, r_first(c) + 1, lambda k: rz(c, k).wait_send())
        if c == 1:

            @pl.when(jnp.logical_not(holds))
            def _():
                rz(c, 0).wait_send()

    by_core(sends)

    @pl.when(holds)
    def _():
        for i, j in far_first:
            f1(i, j, False).wait_send()

    for done in stores:
        done.wait()
    store.wait()


def hand_over(*refs):
    for src, dst in zip(refs[:3], refs[3:]):
        dst[...] = src[...]


def local(q_nope, q_rope, kv_cache, kv_gain, w_uk, w_uv, attn_out, d_out, span_table):
    toks = q_nope.shape[0]
    hbm = pl.BlockSpec(memory_space=pl.ANY)
    smem = pl.BlockSpec(memory_space=pltpu.SMEM)
    vmem = pl.BlockSpec(memory_space=pltpu.VMEM)
    dma = pltpu.SemaphoreType.DMA
    inputs = (
        q_nope, q_rope, kv_cache.T, kv_gain, w_uk, w_uv, attn_out, d_out
    )
    out_shape = (
        jax.ShapeDtypeStruct((toks, HEADS * NOPE), bf16),
        jax.ShapeDtypeStruct((toks, HEADS * ROPE), bf16),
        jax.ShapeDtypeStruct((CAT, toks), f32),
    )
    scratch = [pltpu.VMEM(value.shape, value.dtype) for value in inputs]
    scratch += [pltpu.VMEM(value.shape, value.dtype) for value in out_shape]
    scratch += [
        pltpu.VMEM((NZ, NP, NP, PIECE, CAT), bf16),
        pltpu.VMEM((NZ, NP, NP, PIECE, CAT), bf16),
        pltpu.VMEM((HALF + 1, NP, NP, PIECE, CAT), bf16),
        pltpu.VMEM((HALF + 1, 3, NP, PIECE, CAT), bf16),
        pltpu.VMEM((HALF + 1, 3, PIECE, CAT), bf16),
        pltpu.VMEM((2, HALF + 1, PIECE, CAT), bf16),
        pltpu.VMEM((2, NP, NP, PIECE, CAT), bf16),
        pltpu.VMEM((PIECE, CAT), f32),
        pltpu.VMEM((2, NP, PIECE, CAT), bf16),
        pltpu.VMEM((2, ROWS, CAT), bf16),
        pltpu.VMEM((2, ROWS, LAT), bf16),
        pltpu.VMEM((2, 1, ROWS), f32),
        pltpu.VMEM((FIRST + OTHER, CHUNK, ROWS), f32),
        pltpu.VMEM((FIRST, CHUNK, ROWS), f32),
        pltpu.VMEM((HIDDEN + 1, SPAN, ROWS), f32),
        pltpu.VMEM((HIDDEN + 1, SPAN, ROWS), f32),
        pltpu.VMEM((2, 8, ROWS), f32),
        pltpu.VMEM((BLANK + 1, SPAN, CAT), f32),
        pltpu.VMEM((OTHER, ROWS, CAT), f32),
        pltpu.VMEM((ROWS, CAT), f32),
        pltpu.VMEM((2, 1, ROWS), f32),
        pltpu.VMEM((FIRST + OTHER, 8, ROWS), f32),
        pltpu.VMEM((2 * SPAN, LAT), f32),
        pltpu.VMEM((2 * SPAN, 1), f32),
        pltpu.SMEM((2 * NZ,), jnp.int32),
        dma((len(inputs),)),
        dma((3,)),
        dma((2,)), dma((2,)),
        dma((HALF + 1,)), dma((HALF + 1,)),
        dma((HALF + 1, NP)), dma((HALF + 1, NP)),
        dma((HALF + 1, NP)), dma((HALF + 1, NP)),
        dma((HALF + 1,)), dma((HALF + 1,)),
        dma((HALF + 1,)), dma((HALF + 1,)),
        dma((HALF + 1, NP)), dma((HALF + 1, NP)),
        dma((HALF + 1, NP)), dma((HALF + 1, NP)),
        dma((HALF + 1,)), dma((2, HALF + 1)),
        dma((1,)), dma((2,)),
        dma((NP, NP)), dma((NP, NP)),
    ]
    results = pl.pallas_call(
        kernel,
        out_shape=out_shape,
        in_specs=[hbm] * len(inputs) + [smem],
        out_specs=(hbm, hbm, hbm),
        scratch_shapes=scratch,
        compiler_params=pltpu.CompilerParams(
            collective_id=0, has_side_effects=True, vmem_limit_bytes=60 * 1024 * 1024
        ),
    )(*inputs, span_table.T)
    d_q_nope, d_q_rope, d_cache = pl.pallas_call(
        hand_over,
        out_shape=out_shape,
        in_specs=[vmem] * 3,
        out_specs=(vmem, vmem, vmem),
        compiler_params=pltpu.CompilerParams(vmem_limit_bytes=60 * 1024 * 1024),
    )(*results)
    return d_q_nope, d_q_rope, d_cache.T


def solution(mesh):
    in_specs = (
        P("ctx", "head"),
        P("ctx", "head"),
        P("ctx", None),
        P(),
        P("head", None, None),
        P("head", None, None),
        P("ctx", "head"),
        P("ctx", "head"),
        P(),
    )
    out_specs = (P("ctx", "head"), P("ctx", "head"), P("ctx", None))
    return jax.shard_map(local, mesh=mesh, in_specs=in_specs, out_specs=out_specs, check_vma=False)
```
